256 devices in a mesh: row: 8 (over x, core), col: 32 (over y, z).
Axes of the slice: x: 4, y: 4, z: 8, core: 2. Of those that a mesh axis runs over, the one named last changes fastest.
Arguments:
- sources: bfloat16 [32768, 768], P(('row', 'col')), may hold values from -2 to 2
- targets: bfloat16 [32768, 768], P(('col', 'row')), may hold values from -2 to 2
- projection: bfloat16 [768, 768], replicated, may hold values from -0.21875 to 0.21875
- language: int32 [32768], replicated, may hold values from 0 to 108
- lang_allow: int32 [109, 109], replicated, may hold values 0 or 1
- tile_allow: int32 [64, 64], replicated, may hold values 0 or 1
Outputs:
- grad_sources: bfloat16 [32768, 768], P(('row', 'col'))
- grad_targets: bfloat16 [32768, 768], P(('col', 'row'))
- grad_proj: float32 [768, 768], replicated
The draws below stay inside these ranges and needn't reach their ends.
All inputs are finite; a program needn't handle non-finite values.
Results may differ from the reference program's by a relative error of at most 0.0035.
The reference program's roundings to bfloat16 on the way (of `logit_grad`) count: a program that leaves them out, or rounds other values in their place, can miss the bound.
Values may be sent and summed in bfloat16 or wider, within the bound.
No kernel may reach another device: no remote copies, remote signals or barrier semaphores. Data moves between devices by JAX's collectives and lax.ppermute only.
A program may use at most 128 MiB of HBM per device.

```python
import math
import jax
import jax.numpy as jnp
from jax import lax

D = 768
NL = 109
TILE = 512
PAIRS = 32768
NT = 64


def pair_parts(key):
    key_topic, key_centre, key_own, key_strength = jax.random.split(key, 4)
    topic_count = min(64, max(PAIRS // 8, 1))
    topic = jax.random.randint(key_topic, (PAIRS,), 0, topic_count)
    centres = jax.random.normal(key_centre, (topic_count, D), jnp.float32)
    own = jax.random.normal(key_own, (PAIRS, D), jnp.float32)
    strength = jax.random.uniform(key_strength, (PAIRS, 1), jnp.float32, 0.15, 0.85)
    base = strength * centres[topic]
    rest = jnp.sqrt(1.0 - strength * strength)
    return (base, own, rest)


def draw_sources(key, part):
    base, own, rest = pair_parts(key)
    values = base + rest * own
    values = jnp.clip(values * D ** (-0.5), -2.0, 2.0)
    return values.astype(jnp.bfloat16)


def draw_targets(key, part):
    own_key = jax.random.fold_in(key, 23)
    base, own, rest = pair_parts(key)
    noise_key = jax.random.fold_in(own_key, 0)
    noise = jax.random.normal(noise_key, (PAIRS, D), jnp.float32)
    values = base + rest * (0.92 * own + 0.39 * noise)
    values = jnp.clip(values * D ** (-0.5), -2.0, 2.0)
    return values.astype(jnp.bfloat16)


def touch_ends(entries, key, low, high):
    longest = entries.shape.index(max(entries.shape))
    spots = []
    for shift in (0, 1):
        where = [jax.random.randint(jax.random.fold_in(key, axis), (), 0, length) for axis, length in enumerate(entries.shape)]
        where[longest] = (where[longest] + shift) % entries.shape[longest]
        spots.append(tuple(where))
    return entries.at[spots[0]].set(low).at[spots[1]].set(high)


def normal_values(rng, extent, scale, limit, held_as=jnp.bfloat16):
    array = jax.random.normal(rng, extent, jnp.float32) * scale
    return jnp.minimum(jnp.maximum(array, -limit), limit).astype(held_as)


def setup_inputs(seed: int = 0) -> dict:
    arg_keys = jax.random.split(jax.random.key(seed), 7)
    sources = draw_sources(jax.random.fold_in(arg_keys[6], 71), 0)
    targets = draw_targets(jax.random.fold_in(arg_keys[6], 71), 0)
    projection = normal_values(arg_keys[2], (D, D), D ** -0.5, 0.21875)
    language = touch_ends(jax.random.randint(arg_keys[3], (PAIRS,), 0, NL), jax.random.fold_in(arg_keys[3], 1), 0, NL - 1).astype(jnp.int32)
    lang_allow = touch_ends((jax.random.randint(arg_keys[4], (NL, NL), 0, 4) < 3).astype(jnp.int32), jax.random.fold_in(arg_keys[4], 1), 0, 1)
    tile_allow = touch_ends((jax.random.randint(arg_keys[5], (NT, NT), 0, 2) < 1).astype(jnp.int32), jax.random.fold_in(arg_keys[5], 1), 0, 1)
    return {"sources": sources, "targets": targets, "projection": projection, "language": language, "lang_allow": lang_allow, "tile_allow": tile_allow}


SCALE = 20.0
MARGIN = 0.3

def embedded(inputs, projection):
    raw_proj = jnp.dot(inputs, projection, preferred_element_type=jnp.float32)
    length = jnp.sqrt(lax.optimization_barrier(jnp.sum(raw_proj * raw_proj, axis=-1, keepdims=True)) + 1e-06)
    return (raw_proj, length)

def permitted(row_index, col_index, language, lang_allow, tile_allow):
    tile_ok = tile_allow[row_index // TILE][:, col_index // TILE] == 1
    pair_ok = lang_allow[language[row_index]][:, language[col_index]] == 1
    return tile_ok & pair_ok | (row_index[:, None] == col_index[None, :])

def scaled_logits(row_block, col_emb, row_index, col_index):
    similar = jnp.dot(row_block, col_emb.T, preferred_element_type=jnp.float32)
    diagonal = (row_index[:, None] == col_index[None, :]).astype(jnp.float32)
    return SCALE * (similar - MARGIN * diagonal)

def backward_proj(inputs, raw_proj, length, upstream, projection):
    unit_vec = raw_proj / length
    dir_grad = ((upstream - unit_vec * lax.optimization_barrier(jnp.sum(unit_vec * upstream, axis=-1, keepdims=True))) / length).astype(jnp.bfloat16)
    grad_in = jnp.dot(dir_grad, projection.T, preferred_element_type=jnp.float32).astype(jnp.bfloat16)
    grad_weight = jnp.dot(inputs.T, dir_grad, preferred_element_type=jnp.float32)
    return (grad_in, grad_weight)

def reference(sources, targets, projection, language, lang_allow, tile_allow):
    src_raw, src_len = embedded(sources, projection)
    tgt_raw, tgt_len = embedded(targets, projection)
    src_unit = (src_raw / src_len).astype(jnp.bfloat16)
    tgt_unit = (tgt_raw / tgt_len).astype(jnp.bfloat16)
    block_rows = math.gcd(PAIRS, 1024)
    count_blocks = PAIRS // block_rows
    blocks = src_unit.reshape(count_blocks, block_rows, D)
    starts = (jnp.arange(count_blocks) * block_rows).astype(jnp.int32)
    col_index = jnp.arange(PAIRS).astype(jnp.int32)

    def first_pass(col_total, element):
        row_block, first_row = element
        row_index = first_row + jnp.arange(block_rows).astype(jnp.int32)
        logits = scaled_logits(row_block, tgt_unit, row_index, col_index)
        allowed = permitted(row_index, col_index, language, lang_allow, tile_allow)
        weights = jnp.where(allowed, jnp.exp(logits - SCALE), jnp.float32(0.0))
        return (col_total + lax.optimization_barrier(jnp.sum(weights, axis=0)), lax.optimization_barrier(jnp.sum(weights, axis=1)))
    col_total, row_total = lax.scan(first_pass, jnp.zeros((PAIRS,), jnp.float32), (blocks, starts))
    row_lse = jnp.log(row_total.reshape(PAIRS)) + SCALE
    col_lse = jnp.log(col_total) + SCALE
    lse_blocks = row_lse.reshape(count_blocks, block_rows)

    def second_pass(tgt_grad, element):
        row_block, first_row, lse_rows = element
        row_index = first_row + jnp.arange(block_rows).astype(jnp.int32)
        logits = scaled_logits(row_block, tgt_unit, row_index, col_index)
        allowed = permitted(row_index, col_index, language, lang_allow, tile_allow)
        soft_rows = jnp.where(allowed, jnp.exp(logits - lse_rows[:, None]), jnp.float32(0.0))
        soft_cols = jnp.where(allowed, jnp.exp(logits - col_lse[None, :]), jnp.float32(0.0))
        diagonal = (row_index[:, None] == col_index[None, :]).astype(jnp.float32)
        logit_grad = (SCALE * (0.5 * (soft_rows + soft_cols) - diagonal)).astype(jnp.bfloat16)
        src_part = jnp.dot(logit_grad, tgt_unit, preferred_element_type=jnp.float32)
        tgt_grad = tgt_grad + lax.dot_general(logit_grad, row_block, (((0,), (0,)), ((), ())), preferred_element_type=jnp.float32)
        return (tgt_grad, src_part)
    tgt_grad, src_parts = lax.scan(second_pass, jnp.zeros((PAIRS, D), jnp.float32), (blocks, starts, lse_blocks))
    src_grad = src_parts.reshape(PAIRS, D)
    grad_sources, weight_src = backward_proj(sources, src_raw, src_len, src_grad, projection)
    grad_targets, weight_tgt = backward_proj(targets, tgt_raw, tgt_len, tgt_grad, projection)
    return (grad_sources, grad_targets, weight_src + weight_tgt)
```

```python
import math
import functools
import jax
import jax.numpy as jnp
from jax import lax
from jax.experimental import pallas as pl
from jax.experimental.pallas import tpu as pltpu
from jax.sharding import Mesh, PartitionSpec as P

NX, NC, NY, NZ = 4, 2, 4, 8
AXES = ("x", "core", "y", "z")
SHARD = 128
SLOTS = 16
SIDE = SLOTS * SHARD
TILE = 512
SCALE = 20.0
MARGIN = 0.3
RATE = SCALE * math.log2(math.e)
PENALTY = 64.0
LANGS = 128
EXTRA = 256
REL = (0, 1, 3, 2)
ZREL = (0, 1, 7, 2, 6, 3, 5, 4)
VMEM = 16 * 2**20
bf16 = jnp.bfloat16
f32 = jnp.float32


def device(x, c, y, z):
    return ((x * NC + c) * NY + y) * NZ + z


def send(value, target):
    pairs = []
    for x in range(NX):
        for c in range(NC):
            for y in range(NY):
                for z in range(NZ):
                    pairs.append((device(x, c, y, z), device(*target(x, c, y, z))))
    return lax.ppermute(value, AXES, pairs)


def send_first(value, d):
    return send(value, lambda x, c, y, z: (x, c, (y + d) % NY, z) if c else ((x + d) % NX, c, y, z))


def send_second(value, d):
    return send(value, lambda x, c, y, z: ((x + d) % NX, c, y, z) if c else (x, c, (y + d) % NY, z))


def send_z(value, d):
    return send(value, lambda x, c, y, z: (x, c, y, (z + d) % NZ))


def send_core(value):
    return send(value, lambda x, c, y, z: (x, 1 - c, y, z))


def swap(value, axis, bit):
    def target(x, c, y, z):
        place = dict(x=x, core=c, y=y, z=z)
        place[axis] ^= bit
        return tuple(place[name] for name in AXES)

    return send(value, target)


def together(*values):
    return lax.optimization_barrier(values)


def embed_kernel(x_ref, w_ref, raw_ref, unit_ref):
    raw = jnp.dot(x_ref[...], w_ref[...], preferred_element_type=f32)
    raw_ref[...] = raw
    length = jnp.sqrt(jnp.sum(raw * raw, axis=-1, keepdims=True) + 1e-06)
    unit_ref[...] = (raw / length).astype(bf16)


def embedded(inputs, projection):
    return pl.pallas_call(
        embed_kernel,
        out_shape=[
            jax.ShapeDtypeStruct(inputs.shape, f32),
            jax.ShapeDtypeStruct(inputs.shape, bf16),
        ],
        compiler_params=pltpu.CompilerParams(vmem_limit_bytes=VMEM),
        name="embed",
    )(inputs, projection)


def join_kernel(*refs):
    pieces, out = refs[:-1], refs[-1]
    first = 0
    for piece in pieces:
        count = piece.shape[0]
        out[first : first + count, :] = piece[...]
        first += count


def join(*pieces):
    count = sum(piece.shape[0] for piece in pieces)
    return pl.pallas_call(
        join_kernel,
        out_shape=jax.ShapeDtypeStruct((count,) + pieces[0].shape[1:], pieces[0].dtype),
        name="join",
    )(*pieces)


def gather_rows(own):
    half = own.shape[0] // 2
    p, m = together(send_first(own, -1), send_first(own, 1))
    q0, q1 = together(send_first(p[:half], -1), send_first(m[half:], 1))
    line = join(own, p, m, q0, q1)
    half = line.shape[0] // 2
    p, m = together(send_second(line, -1), send_second(line, 1))
    return line, p, m, send_second(p[:half], -1), send_second(m[half:], 1)


def plus(a, b, dtype=bf16):
    return (a.astype(f32) + b.astype(f32)).astype(dtype)


def scatter_rest(b0, up, down, mine, other):
    mine = mine + other
    far = mine[7].astype(bf16)
    rise, fall = together(send_z(far[:384], 1), send_z(far[384:], -1))
    rise = jnp.concatenate([plus(mine[5][:384], rise), mine[5][384:].astype(bf16)], axis=0)
    fall = jnp.concatenate([mine[6][:384].astype(bf16), plus(mine[6][384:], fall)], axis=0)
    rise, fall, up, down = together(send_z(rise, 1), send_z(fall, -1), up, down)
    b0 = b0 + up + down
    b0, b1, b3, b2 = (b0[k * 128 : (k + 1) * 128] for k in range(4))
    rise = plus(mine[3], rise, f32)
    fall = plus(mine[4], fall, f32)
    up, down, rise, fall = together(
        send_first(b2[:64], 1), send_first(b2[64:], -1), send_z(rise, 1), send_z(fall, -1)
    )
    b1 = jnp.concatenate([b1[:64] + up, b1[64:]], axis=0)
    b3 = jnp.concatenate([b3[:64], b3[64:] + down], axis=0)
    up, down, rise, fall = together(
        send_first(b1, 1), send_first(b3, -1), send_z(mine[1] + rise, 1), send_z(mine[2] + fall, -1)
    )
    return (b0, up, down), (mine[0], rise, fall)


def sum_totals(rows, cols):
    for axis, bit, other_axis, other_bit in (
        ("x", 1, "core", 1),
        ("x", 2, "z", 1),
        ("y", 1, "z", 2),
        ("y", 2, "z", 4),
    ):
        r, c = together(swap(rows, axis, bit), swap(cols, other_axis, other_bit))
        if other_axis == "core":
            c = jnp.concatenate([c[NZ:], c[:NZ]], axis=0)
        rows, cols = rows + r, cols + c
    return rows, cols


def exchange(value, axes):
    return lax.all_to_all(value, axes, split_axis=0, concat_axis=0, tiled=True)


def sum_weight(mine, other, core):
    half, depth = mine.shape
    mine = plus(mine, send_core(other))
    part = half // (NX * NY)
    got = exchange(mine, ("x", "y")).reshape(NX * NY, part, depth)
    mine = jnp.sum(got.astype(f32), axis=0).astype(bf16)
    wide = jnp.broadcast_to(mine[None], (NZ, part, depth)).reshape(NZ * part, depth)
    got = exchange(wide, "z").reshape(NZ, part, depth)
    mine = jnp.sum(got.astype(f32), axis=0).astype(bf16)
    wide = jnp.broadcast_to(mine[None], (NX * NY, part, depth)).reshape(half, depth)
    mine = exchange(wide, ("x", "y"))
    other = send_core(mine)
    low = jnp.where(core == 0, mine, other)
    high = jnp.where(core == 0, other, mine)
    return jnp.concatenate([low, high], axis=0).astype(f32)


def offset_of_diagonal(rows, columns, first):
    lane = lax.broadcasted_iota(jnp.int32, (rows, columns), 1)
    return lane + first - lax.broadcasted_iota(jnp.int32, (rows, columns), 0)


def weigh_kernel(late, dslot, rplace, *refs):
    pieces, refs = refs[:5], refs[5:]
    if late:
        sm_ref, t_ref, tm_ref, e_ref, row_ref, col_ref, s_all, acc = refs
    else:
        sm_ref, t_ref, tm_ref, e_ref, st_ref, row_ref, col_ref, s_all, acc = refs
    step = pl.program_id(0)
    rows = 2 * SHARD

    @pl.when(step == 0)
    def _():
        first = 0
        for piece in pieces:
            count = piece.shape[0]
            s_all[first : first + count, :] = piece[...]
            first += count
        acc[...] = jnp.zeros_like(acc)

    s = s_all[pl.ds(pl.multiple_of(step * rows, rows), rows), :]
    sm = sm_ref[...]
    if not late:
        st_ref[...] = s.T
    sums = [jnp.zeros((SHARD, 128), f32) for _ in range(2)]
    width = 512
    contract = (((1,), (1,)), ((), ()))
    for first in range(0, t_ref.shape[0], width):
        t = t_ref[first : first + width, :]
        tm = tm_ref[first : first + width, :]
        sim = lax.dot_general(s, t, contract, preferred_element_type=f32)
        sim += lax.dot_general(sm, tm, contract, preferred_element_type=f32)
        e = jnp.exp2(sim * RATE - RATE)
        offset = offset_of_diagonal(SHARD, width, first)
        for h in range(2):
            part = e[h * SHARD : (h + 1) * SHARD]
            part = jnp.where(offset == dslot[2 * step + h] * SHARD, 0.0, part)
            e_ref[h * SHARD : (h + 1) * SHARD, first : first + width] = part
            for k in range(0, width, 128):
                sums[h] = sums[h] + part[:, k : k + 128]
            acc[:, first : first + width] += jnp.sum(part.reshape(SHARD // 8, 8, width), axis=0)
    for h in range(2):
        slot = dslot[2 * step + h]
        place = rplace[2 * step + h]
        row_ref[pl.ds(place, 1), :] = jnp.sum(sums[h].T, axis=0, keepdims=True)

        @pl.when(slot >= 0)
        def _():
            here = pl.ds(pl.multiple_of(slot * SHARD, SHARD), SHARD)
            a = s[h * SHARD : (h + 1) * SHARD].astype(f32)
            b = t_ref[here, :].astype(f32)
            sim = jnp.sum(a * b, axis=1, keepdims=True)
            value = jnp.exp2(sim * RATE - (1.0 + MARGIN) * RATE)
            block = jnp.where(offset_of_diagonal(SHARD, SHARD, 0) == 0, value, 0.0)
            e_ref[h * SHARD : (h + 1) * SHARD, here] += block
            line = jnp.sum(block, axis=0, keepdims=True)
            row_ref[pl.ds(place, 1), :] += line
            acc[0:1, here] += line

    @pl.when(step == pl.num_programs(0) - 1)
    def _():
        total = jnp.sum(acc[...], axis=0, keepdims=True)
        for k in range(NZ):
            col_ref[k : k + 1, :] = total[:, k * SHARD : (k + 1) * SHARD]


def weigh(dslot, rplace, pieces, row_mask, cols, col_mask, late):
    depth = cols.shape[1]
    half = cols.shape[0]
    step = 2 * SHARD
    whole = lambda i, *_: (0, 0)
    in_specs = [pl.BlockSpec(v.shape, whole, pipeline_mode=pl.Buffered(1)) for v in pieces] + [
        pl.BlockSpec((step, EXTRA), lambda i, *_: (i, 0)),
        pl.BlockSpec((half, depth), whole),
        pl.BlockSpec((half, EXTRA), whole),
    ]
    out_specs = [
        pl.BlockSpec((step, half), lambda i, *_: (i, 0)),
        pl.BlockSpec((depth, step), lambda i, *_: (0, i)),
        pl.BlockSpec((SLOTS, SHARD), whole),
        pl.BlockSpec((NZ, SHARD), whole),
    ]
    out_shape = [
        jax.ShapeDtypeStruct((SIDE, half), f32),
        jax.ShapeDtypeStruct((depth, SIDE), bf16),
        jax.ShapeDtypeStruct((SLOTS, SHARD), f32),
        jax.ShapeDtypeStruct((NZ, SHARD), f32),
    ]
    if late:
        del out_specs[1], out_shape[1]
    return pl.pallas_call(
        functools.partial(weigh_kernel, late),
        grid_spec=pltpu.PrefetchScalarGridSpec(
            num_scalar_prefetch=2,
            grid=(SIDE // step,),
            in_specs=in_specs,
            out_specs=out_specs,
            scratch_shapes=[
                pltpu.VMEM((SIDE, depth), bf16),
                pltpu.VMEM((8, half), f32),
            ],
        ),
        out_shape=out_shape,
        cost_estimate=pl.CostEstimate(
            flops=2 * SIDE * half * (depth + EXTRA), bytes_accessed=4 * SIDE * half, transcendentals=SIDE * half
        ),
        compiler_params=pltpu.CompilerParams(vmem_limit_bytes=VMEM),
        name="weigh",
    )(dslot, rplace, *pieces, row_mask, cols, col_mask)


def source_kernel(place, dslot, rplace, e0_ref, e1_ref, t0_ref, t1_ref, rt_ref, ct_ref, *refs):
    if place is not None:
        add_ref, refs = refs[0], refs[1:]
    g_ref, out_ref, acc, scale = refs
    step = pl.program_id(0)
    last = pl.num_programs(0) - 1
    rows, width = e0_ref.shape
    per_step = width // SHARD

    @pl.when(step == 0)
    def _():
        for h in range(rows // SHARD):
            row = (0.5 * SCALE) / rt_ref[pl.ds(rplace[h], 1), :]
            scale[h * SHARD : (h + 1) * SHARD, :] = jnp.broadcast_to(row, (SHARD, SHARD)).T
        acc[...] = jnp.zeros_like(acc)

    def work(e_ref, t_ref):
        eye = jnp.where(offset_of_diagonal(SHARD, SHARD, 0) == 0, SCALE, 0.0)
        for k in range(per_step):
            slot = step * per_step + k
            here = slice(k * SHARD, (k + 1) * SHARD)
            col = (0.5 * SCALE) / ct_ref[pl.ds(slot, 1), :]
            for h in range(rows // SHARD):
                there = slice(h * SHARD, (h + 1) * SHARD)
                g = e_ref[there, here] * (scale[there, :] + col)
                g = g - eye * (dslot[h] == slot).astype(f32)
                g_ref[there, here] = g.astype(bf16)
        acc[...] += jnp.dot(g_ref[...], t_ref[...], preferred_element_type=f32)

    pl.when(step <= last // 2)(lambda: work(e0_ref, t0_ref))
    pl.when(step > last // 2)(lambda: work(e1_ref, t1_ref))

    @pl.when(step == last)
    def _():
        if place is None:
            out_ref[...] = acc[...].astype(out_ref.dtype)
        else:
            half = rows // 2
            there = slice(half - place, 2 * half - place)
            here = slice(place, place + half)
            out_ref[there, :] = acc[there, :].astype(out_ref.dtype)
            out_ref[here, :] = (acc[here, :] + add_ref[...].astype(f32)).astype(out_ref.dtype)


def source_terms(dslot, rplace, block, e, cols, row_total, col_total, dtype, add=None, place=None):
    depth = cols[0].shape[1]
    rows, width = 512, 512
    steps = SIDE // width
    whole = lambda i, *_: (0, 0)
    early = lambda i: jnp.minimum(i, steps // 2 - 1)
    late = lambda i: jnp.maximum(i - steps // 2, 0)
    in_specs = [
        pl.BlockSpec((rows, width), lambda i, *_: (block, early(i))),
        pl.BlockSpec((rows, width), lambda i, *_: (block, late(i))),
        pl.BlockSpec((width, depth), lambda i, *_: (early(i), 0)),
        pl.BlockSpec((width, depth), lambda i, *_: (late(i), 0)),
        pl.BlockSpec((SLOTS, SHARD), whole),
        pl.BlockSpec((SLOTS, SHARD), whole),
    ]
    some = lambda v: lax.slice_in_dim(v, 4 * block, 4 * block + 4)
    args = [some(dslot), some(rplace), *e, *cols, row_total, col_total]
    if place is not None:
        in_specs.append(pl.BlockSpec(add.shape, whole))
        args.append(add)
    return pl.pallas_call(
        functools.partial(source_kernel, place),
        grid_spec=pltpu.PrefetchScalarGridSpec(
            num_scalar_prefetch=2,
            grid=(steps,),
            in_specs=in_specs,
            out_specs=[
                pl.BlockSpec((rows, width), lambda i, *_: (0, i)),
                pl.BlockSpec((rows, depth), whole),
            ],
            scratch_shapes=[pltpu.VMEM((rows, depth), f32), pltpu.VMEM((rows, SHARD), f32)],
        ),
        out_shape=[
            jax.ShapeDtypeStruct((rows, SIDE), bf16),
            jax.ShapeDtypeStruct((rows, depth), dtype),
        ],
        cost_estimate=pl.CostEstimate(
            flops=2 * rows * SIDE * depth, bytes_accessed=6 * rows * SIDE, transcendentals=0
        ),
        compiler_params=pltpu.CompilerParams(vmem_limit_bytes=VMEM),
        name="source_terms",
    )(*args)


def target_kernel(zplace, st_ref, g0, g1, g3, g2, out_ref):
    step = pl.program_id(0)
    got = None
    for k, g_ref in enumerate((g0, g1, g3, g2)):
        rows = g_ref.shape[0]
        term = jnp.dot(st_ref[:, k * rows : (k + 1) * rows], g_ref[...], preferred_element_type=f32)
        got = term if got is None else got + term
    for k in range(2):
        out_ref[zplace[2 * step + k]] = got[:, k * SHARD : (k + 1) * SHARD]


def target_terms(zplace, half, rows_t, g):
    depth = rows_t.shape[0]
    width = 2 * SHARD
    steps = SIDE // 2 // width
    return pl.pallas_call(
        target_kernel,
        grid_spec=pltpu.PrefetchScalarGridSpec(
            num_scalar_prefetch=1,
            grid=(steps,),
            in_specs=[pl.BlockSpec((depth, SIDE), lambda i, *_: (0, 0))]
            + [pl.BlockSpec((512, width), lambda i, *_: (0, half * steps + i))] * 4,
            out_specs=pl.BlockSpec((NZ, depth, SHARD), lambda i, *_: (0, 0, 0)),
        ),
        out_shape=jax.ShapeDtypeStruct((NZ, depth, SHARD), f32),
        cost_estimate=pl.CostEstimate(
            flops=SIDE * SIDE * depth, bytes_accessed=SIDE * SIDE, transcendentals=0
        ),
        compiler_params=pltpu.CompilerParams(vmem_limit_bytes=VMEM),
        name="target_terms",
    )(zplace, rows_t, *g)


def two_hot(shards, language):
    lang = jnp.take(language.reshape(-1, SHARD), shards, axis=0)[..., None]
    tile = (shards // (TILE // SHARD))[:, None, None] + LANGS
    lane = jnp.arange(EXTRA, dtype=jnp.int32)[None, None, :]
    hot = (lane == lang) | (lane == tile)
    return hot.astype(bf16).reshape(shards.shape[0] * SHARD, EXTRA)


def penalties(lang_allow, tile_allow):
    langs, tiles = lang_allow.shape[0], tile_allow.shape[0]
    lang = jnp.where(lang_allow == 1, 0.0, -PENALTY).astype(bf16).T
    tile = jnp.where(tile_allow == 1, 0.0, -PENALTY).astype(bf16).T
    rest = EXTRA - LANGS - tiles
    return jnp.pad(lang, ((0, EXTRA - langs), (0, EXTRA - langs))) + jnp.pad(
        tile, ((LANGS, rest), (LANGS, rest))
    )


def backward_kernel(flip, x_ref, raw_ref, w_ref, term0, term1, term2, *refs):

    grad = term0[...] + term1[...] + term2[...]
    if flip:
        grad = grad.T
    raw = raw_ref[...]
    length = jnp.sqrt(jnp.sum(raw * raw, axis=-1, keepdims=True) + 1e-06)
    unit = raw / length
    turn = grad - unit * jnp.sum(unit * grad, axis=-1, keepdims=True)
    turn = (turn / length).astype(bf16)
    contract = (((1,), (1,)), ((), ()))
    weight = jnp.dot(x_ref[...].T, turn, preferred_element_type=f32)
    if flip:
        core, before, out_ref, mine_ref, other_ref, whole = refs
        whole[...] = weight + before[...]
        size = mine_ref.shape[0]
        first = pl.multiple_of(core[0] * size, size)
        mine_ref[...] = whole[pl.ds(first, size), :]
        other_ref[...] = whole[pl.ds(size - first, size), :].astype(bf16)
    else:
        out_ref, weight_ref = refs
        weight_ref[...] = weight
    out_ref[...] = lax.dot_general(turn, w_ref[...], contract, preferred_element_type=f32).astype(bf16)


def backward(inputs, raw, projection, terms, core=None, before=None):
    flip = before is not None
    depth = inputs.shape[1]
    args = [inputs, raw, projection, *terms]
    in_specs = [pl.BlockSpec(memory_space=pltpu.VMEM)] * len(args)
    out_shape = [jax.ShapeDtypeStruct(inputs.shape, bf16)]
    scratch = []
    if flip:
        args += [core.reshape(1), before]
        in_specs += [pl.BlockSpec(memory_space=pltpu.SMEM), pl.BlockSpec(memory_space=pltpu.VMEM)]
        out_shape += [
            jax.ShapeDtypeStruct((depth // 2, depth), f32),
            jax.ShapeDtypeStruct((depth // 2, depth), bf16),
        ]
        scratch = [pltpu.VMEM((depth, depth), f32)]
    else:
        out_shape += [jax.ShapeDtypeStruct((depth, depth), f32)]
    return pl.pallas_call(
        functools.partial(backward_kernel, flip),
        in_specs=in_specs,
        out_shape=out_shape,
        scratch_shapes=scratch,
        cost_estimate=pl.CostEstimate(
            flops=4 * SHARD * depth * depth, bytes_accessed=6 * depth * depth, transcendentals=0
        ),
        compiler_params=pltpu.CompilerParams(vmem_limit_bytes=VMEM),
        name="backward",
    )(*args)


def per_device(sources, targets, projection, language, lang_allow, tile_allow):
    x, core, y, z = (lax.axis_index(name) for name in AXES)
    rel = jnp.array(REL, jnp.int32)
    first, second = jnp.tile(rel, 4), jnp.repeat(rel, 4)
    row_x = (x + jnp.where(core == 0, first, second)) % NX
    row_y = (y + jnp.where(core == 0, second, first)) % NY
    row_shard = row_x * 64 + core * 32 + row_y * 8 + z
    row_place = row_x * NY + row_y
    col_z = jnp.arange(NZ, dtype=jnp.int32)
    col_shards = [y * 64 + col_z * 8 + x * 2 + c for c in (core, 1 - core)]
    dslots = [
        jnp.max(jnp.where(row_shard[:, None] == shards[None, :], col_z[None, :], -1), axis=1)
        for shards in col_shards
    ]
    z_place = jnp.sum(
        jnp.where(
            (z + jnp.array(ZREL, jnp.int32))[None, :] % NZ == col_z[:, None], col_z[None, :], 0
        ),
        axis=1,
    )

    tgt_raw, tgt_unit = embedded(targets, projection)
    mine = lax.all_gather(tgt_unit, "z", axis=0, tiled=True)
    src_raw, src_unit = embedded(sources, projection)
    cost = penalties(lang_allow, tile_allow)
    row_mask = two_hot(row_shard, language)
    col_masks = [
        jnp.dot(two_hot(shards, language), cost, preferred_element_type=f32).astype(bf16)
        for shards in col_shards
    ]
    pieces = gather_rows(src_unit)
    mine, *pieces = together(mine, *pieces)
    other = send_core(mine)

    e0, rows_t, row0, col0 = weigh(dslots[0], row_place, pieces, row_mask, mine, col_masks[0], False)
    e1, row1, col1 = weigh(dslots[1], row_place, pieces, row_mask, other, col_masks[1], True)
    row_total, col_total = sum_totals(row0 + row1, jnp.concatenate([col0, col1], axis=0))

    dslot = jnp.where(dslots[1] >= 0, dslots[1] + NZ, dslots[0])
    terms = lambda block, dtype, *add: source_terms(
        dslot, row_place, block, (e0, e1), (mine, other), row_total, col_total, dtype, *add
    )
    g2, o2 = terms(3, bf16)
    row_place, o2 = together(row_place, o2)
    up, down = send_second(o2[:256], 1), send_second(o2[256:], -1)
    g0, o0 = terms(0, f32)
    g1, o1 = terms(1, f32, up, 0)
    g3, o3 = terms(2, f32, down, 256)
    up, down = send_second(o1, 1), send_second(o3, -1)
    tgt_other = target_terms(z_place, 1, rows_t, (g0, g1, g3, g2))
    z_place, tgt_other = together(z_place, tgt_other)
    tgt_mine = target_terms(z_place, 0, rows_t, (g0, g1, g3, g2))
    src_parts, tgt_parts = scatter_rest(o0, up, down, tgt_mine, send_core(tgt_other))

    grad_sources, weight = backward(sources, src_raw, projection, src_parts)
    grad_targets, half, half_other = backward(targets, tgt_raw, projection, tgt_parts, core, weight)
    return (grad_sources, grad_targets, sum_weight(half, half_other, core))


def solution(mesh):
    fine = Mesh(mesh.devices.reshape(NX, NC, NY, NZ), AXES)
    return jax.shard_map(
        per_device,
        mesh=fine,
        in_specs=(P(("x", "core", "y", "z"), None), P(("y", "z", "x", "core"), None), P(), P(), P(), P()),
        out_specs=(P(("x", "core", "y", "z"), None), P(("y", "z", "x", "core"), None), P()),
        check_vma=False,
    )
```

```python
import math
import functools
import jax
import jax.numpy as jnp
from jax import lax
from jax.experimental import pallas as pl
from jax.experimental.pallas import tpu as pltpu
from jax.sharding import Mesh, PartitionSpec as P

NX, NC, NY, NZ = 4, 2, 4, 8
AXES = ("x", "core", "y", "z")
SHARD = 128
SLOTS = 16
SIDE = SLOTS * SHARD
TILE = 512
SCALE = 20.0
MARGIN = 0.3
RATE = SCALE * math.log2(math.e)
PENALTY = 64.0
LANGS = 128
EXTRA = 256
REL = (0, 1, 3, 2)
ZREL = (0, 1, 7, 2, 6, 3, 5, 4)
VMEM = 16 * 2**20
bf16 = jnp.bfloat16
f32 = jnp.float32


def device(x, c, y, z):
    return ((x * NC + c) * NY + y) * NZ + z


def send(value, target):
    pairs = []
    for x in range(NX):
        for c in range(NC):
            for y in range(NY):
                for z in range(NZ):
                    pairs.append((device(x, c, y, z), device(*target(x, c, y, z))))
    return lax.ppermute(value, AXES, pairs)


def send_first(value, d):
    return send(value, lambda x, c, y, z: (x, c, (y + d) % NY, z) if c else ((x + d) % NX, c, y, z))


def send_second(value, d):
    return send(value, lambda x, c, y, z: ((x + d) % NX, c, y, z) if c else (x, c, (y + d) % NY, z))


def send_z(value, d):
    return send(value, lambda x, c, y, z: (x, c, y, (z + d) % NZ))


def send_core(value):
    return send(value, lambda x, c, y, z: (x, 1 - c, y, z))


def swap(value, axis, bit):
    def target(x, c, y, z):
        place = dict(x=x, core=c, y=y, z=z)
        place[axis] ^= bit
        return tuple(place[name] for name in AXES)

    return send(value, target)


def together(*values):
    return lax.optimization_barrier(values)


def project(x, w_ref):
    raw = jnp.dot(x, w_ref[...], preferred_element_type=f32)
    length = jnp.sqrt(jnp.sum(raw * raw, axis=-1, keepdims=True) + 1e-06)
    return raw, length


def embed_kernel(lanes, count, *refs):
    pieces, w_ref, refs = refs[:count], refs[count], refs[count + 1 :]
    unit_ref, inv_ref = refs[:2]
    first = 0
    for piece in pieces:
        rows = piece.shape[0]
        here = slice(first, first + rows)
        x = piece[...]
        if count > 1:
            refs[2][here, :] = x
        raw, length = project(x, w_ref)
        unit_ref[here, :] = (raw / length).astype(bf16)
        inv = jnp.broadcast_to(1.0 / length, (rows, SHARD))
        if lanes:
            for k in range(rows // SHARD):
                inv_ref[k : k + 1, :] = inv[k * SHARD : (k + 1) * SHARD].T[:1]
        else:
            inv_ref[here, :] = inv
        first += rows


def embed(projection, *pieces, lanes=False):
    rows = sum(piece.shape[0] for piece in pieces)
    depth = projection.shape[0]
    out_shape = [
        jax.ShapeDtypeStruct((rows, depth), bf16),
        jax.ShapeDtypeStruct((rows // SHARD if lanes else rows, SHARD), f32),
    ]
    if len(pieces) > 1:
        out_shape.append(jax.ShapeDtypeStruct((rows, depth), bf16))
    return pl.pallas_call(
        functools.partial(embed_kernel, lanes, len(pieces)),
        out_shape=out_shape,
        cost_estimate=pl.CostEstimate(
            flops=2 * rows * depth * depth, bytes_accessed=4 * rows * depth, transcendentals=0
        ),
        compiler_params=pltpu.CompilerParams(vmem_limit_bytes=VMEM),
        name="embed",
    )(*pieces, projection)


def join_kernel(*refs):
    pieces, out = refs[:-1], refs[-1]
    first = 0
    for piece in pieces:
        count = piece.shape[0]
        out[first : first + count, :] = piece[...]
        first += count


def join(*pieces):
    count = sum(piece.shape[0] for piece in pieces)
    return pl.pallas_call(
        join_kernel,
        out_shape=jax.ShapeDtypeStruct((count,) + pieces[0].shape[1:], pieces[0].dtype),
        name="join",
    )(*pieces)


def gather_rows(own, projection):
    half = own.shape[0] // 2
    p, m = together(send_first(own, -1), send_first(own, 1))
    q0, q1 = together(send_first(p[:half], -1), send_first(m[half:], 1))
    line = join(own, p, m, q0, q1)
    half = line.shape[0] // 2
    p, m, *first = together(
        send_second(line, -1), send_second(line, 1), *embed(projection, line)
    )
    q0, q1, *rest = together(
        send_second(p[:half], -1),
        send_second(m[half:], 1),
        *embed(projection, p),
        *embed(projection, m),
    )
    units, invs = (first[0], rest[0], rest[2]), (first[1], rest[1], rest[3])
    return (line, p, m, q0, q1), units, invs


def plus(a, b, dtype=bf16):
    return (a.astype(f32) + b.astype(f32)).astype(dtype)


def exchange(value, axes):
    return lax.all_to_all(value, axes, split_axis=0, concat_axis=0, tiled=True)


def scatter_rest(b0, up, down, mine, other, core, weights):
    mine = mine + other
    far = mine[7].astype(bf16)
    rise, fall, weight, weight_other = together(
        send_z(far[:384], 1), send_z(far[384:], -1), *weights()
    )
    rise = jnp.concatenate([plus(mine[5][:384], rise), mine[5][384:].astype(bf16)], axis=0)
    fall = jnp.concatenate([mine[6][:384].astype(bf16), plus(mine[6][384:], fall)], axis=0)
    half, depth = weight.shape
    part = half // (NX * NY)
    rise, fall, up, down, weight_other = together(
        send_z(rise, 1), send_z(fall, -1), up, down, send_core(weight_other)
    )
    weight = plus(weight, weight_other)
    b0 = b0 + up + down
    b0, b1, b3, b2 = (b0[k * 128 : (k + 1) * 128] for k in range(4))
    up, down, rise, fall, got = together(
        send_first(b2[:64], 1),
        send_first(b2[64:], -1),
        send_z(plus(mine[3], rise, f32), 1),
        send_z(plus(mine[4], fall, f32), -1),
        exchange(weight, ("x", "y")),
    )
    weight = jnp.sum(got.reshape(NX * NY, part, depth).astype(f32), axis=0).astype(bf16)
    weight = jnp.broadcast_to(weight[None], (NZ, part, depth)).reshape(NZ * part, depth)
    b1 = jnp.concatenate([b1[:64] + up, b1[64:]], axis=0)
    b3 = jnp.concatenate([b3[:64], b3[64:] + down], axis=0)
    up, down, rise, fall, got = together(
        send_first(b1, 1),
        send_first(b3, -1),
        send_z(mine[1] + rise, 1),
        send_z(mine[2] + fall, -1),
        exchange(weight, "z"),
    )
    weight = jnp.sum(got.reshape(NZ, part, depth).astype(f32), axis=0).astype(bf16)
    weight = jnp.broadcast_to(weight[None], (NX * NY, part, depth)).reshape(half, depth)
    weight = exchange(weight, ("x", "y"))
    other = send_core(weight)
    low = jnp.where(core == 0, weight, other)
    high = jnp.where(core == 0, other, weight)
    grad_proj = jnp.concatenate([low, high], axis=0).astype(f32)
    return (b0, up, down), (mine[0], rise, fall), grad_proj


def sum_totals(rows, cols):
    for axis, bit, other_axis, other_bit in (
        ("x", 1, "core", 1),
        ("x", 2, "z", 1),
        ("y", 1, "z", 2),
        ("y", 2, "z", 4),
    ):
        r, c = together(swap(rows, axis, bit), swap(cols, other_axis, other_bit))
        if other_axis == "core":
            c = jnp.concatenate([c[NZ:], c[:NZ]], axis=0)
        rows, cols = rows + r, cols + c
    return rows, cols


def offset_of_diagonal(rows, columns, first):
    lane = lax.broadcasted_iota(jnp.int32, (rows, columns), 1)
    return lane + first - lax.broadcasted_iota(jnp.int32, (rows, columns), 0)


def weigh_kernel(late, dslot, rplace, *refs):
    pieces, refs = refs[:4], refs[4:]
    if late:
        sm_ref, t_ref, tm_ref, e_ref, row_ref, col_ref, s_all, acc = refs
    else:
        sm_ref, t_ref, tm_ref, e_ref, st_ref, row_ref, col_ref, s_all, acc = refs
    step = pl.program_id(0)
    rows = 2 * SHARD

    @pl.when(step == 0)
    def _():
        first = 0
        for piece in pieces:
            count = piece.shape[0]
            s_all[first : first + count, :] = piece[...]
            first += count
        acc[...] = jnp.zeros_like(acc)

    s = s_all[pl.ds(pl.multiple_of(step * rows, rows), rows), :]
    sm = sm_ref[...]
    if not late:
        st_ref[...] = s.T
    sums = [jnp.zeros((SHARD, 128), f32) for _ in range(2)]
    width = 512
    contract = (((1,), (1,)), ((), ()))
    for first in range(0, t_ref.shape[0], width):
        t = t_ref[first : first + width, :]
        tm = tm_ref[first : first + width, :]
        sim = lax.dot_general(s, t, contract, preferred_element_type=f32)
        sim += lax.dot_general(sm, tm, contract, preferred_element_type=f32)
        e = jnp.exp2(sim * RATE - RATE)
        offset = offset_of_diagonal(SHARD, width, first)
        for h in range(2):
            part = e[h * SHARD : (h + 1) * SHARD]
            part = jnp.where(offset == dslot[2 * step + h] * SHARD, 0.0, part)
            e_ref[h * SHARD : (h + 1) * SHARD, first : first + width] = part
            for k in range(0, width, 128):
                sums[h] = sums[h] + part[:, k : k + 128]
            acc[:, first : first + width] += jnp.sum(part.reshape(SHARD // 8, 8, width), axis=0)
    for h in range(2):
        slot = dslot[2 * step + h]
        place = rplace[2 * step + h]
        row_ref[pl.ds(place, 1), :] = jnp.sum(sums[h].T, axis=0, keepdims=True)

        @pl.when(slot >= 0)
        def _():
            here = pl.ds(pl.multiple_of(slot * SHARD, SHARD), SHARD)
            a = s[h * SHARD : (h + 1) * SHARD].astype(f32)
            b = t_ref[here, :].astype(f32)
            sim = jnp.sum(a * b, axis=1, keepdims=True)
            value = jnp.exp2(sim * RATE - (1.0 + MARGIN) * RATE)
            block = jnp.where(offset_of_diagonal(SHARD, SHARD, 0) == 0, value, 0.0)
            e_ref[h * SHARD : (h + 1) * SHARD, here] += block
            line = jnp.sum(block, axis=0, keepdims=True)
            row_ref[pl.ds(place, 1), :] += line
            acc[0:1, here] += line

    @pl.when(step == pl.num_programs(0) - 1)
    def _():
        total = jnp.sum(acc[...], axis=0, keepdims=True)
        for k in range(NZ):
            col_ref[k : k + 1, :] = total[:, k * SHARD : (k + 1) * SHARD]


def weigh(dslot, rplace, pieces, row_mask, cols, col_mask, late):
    depth = cols.shape[1]
    half = cols.shape[0]
    step = 2 * SHARD
    whole = lambda i, *_: (0, 0)
    in_specs = [pl.BlockSpec(v.shape, whole, pipeline_mode=pl.Buffered(1)) for v in pieces] + [
        pl.BlockSpec((step, EXTRA), lambda i, *_: (i, 0)),
        pl.BlockSpec((half, depth), whole),
        pl.BlockSpec((half, EXTRA), whole),
    ]
    out_specs = [
        pl.BlockSpec((step, half), lambda i, *_: (i, 0)),
        pl.BlockSpec((depth, step), lambda i, *_: (0, i)),
        pl.BlockSpec((SLOTS, SHARD), whole),
        pl.BlockSpec((NZ, SHARD), whole),
    ]
    out_shape = [
        jax.ShapeDtypeStruct((SIDE, half), f32),
        jax.ShapeDtypeStruct((depth, SIDE), bf16),
        jax.ShapeDtypeStruct((SLOTS, SHARD), f32),
        jax.ShapeDtypeStruct((NZ, SHARD), f32),
    ]
    if late:
        del out_specs[1], out_shape[1]
    return pl.pallas_call(
        functools.partial(weigh_kernel, late),
        grid_spec=pltpu.PrefetchScalarGridSpec(
            num_scalar_prefetch=2,
            grid=(SIDE // step,),
            in_specs=in_specs,
            out_specs=out_specs,
            scratch_shapes=[
                pltpu.VMEM((SIDE, depth), bf16),
                pltpu.VMEM((8, half), f32),
            ],
        ),
        out_shape=out_shape,
        cost_estimate=pl.CostEstimate(
            flops=2 * SIDE * half * (depth + EXTRA), bytes_accessed=4 * SIDE * half, transcendentals=SIDE * half
        ),
        compiler_params=pltpu.CompilerParams(vmem_limit_bytes=VMEM),
        name="weigh",
    )(dslot, rplace, *pieces, row_mask, cols, col_mask)


def source_kernel(place, dslot, rplace, e0_ref, e1_ref, t0_ref, t1_ref, rt_ref, ct_ref, s_ref, inv_ref, *refs):
    if place is not None:
        add_ref, refs = refs[0], refs[1:]
    g_ref, out_ref, dir_ref, acc, scale = refs
    step = pl.program_id(0)
    last = pl.num_programs(0) - 1
    rows, width = e0_ref.shape
    per_step = width // SHARD

    @pl.when(step == 0)
    def _():
        for h in range(rows // SHARD):
            row = (0.5 * SCALE) / rt_ref[pl.ds(rplace[h], 1), :]
            scale[h * SHARD : (h + 1) * SHARD, :] = jnp.broadcast_to(row, (SHARD, SHARD)).T
        acc[...] = jnp.zeros_like(acc)

    def work(e_ref, t_ref):
        eye = jnp.where(offset_of_diagonal(SHARD, SHARD, 0) == 0, SCALE, 0.0)
        for k in range(per_step):
            slot = step * per_step + k
            here = slice(k * SHARD, (k + 1) * SHARD)
            col = (0.5 * SCALE) / ct_ref[pl.ds(slot, 1), :]
            for h in range(rows // SHARD):
                there = slice(h * SHARD, (h + 1) * SHARD)
                g = e_ref[there, here] * (scale[there, :] + col)
                g = g - eye * (dslot[h] == slot).astype(f32)
                g_ref[there, here] = g.astype(bf16)
        acc[...] += jnp.dot(g_ref[...], t_ref[...], preferred_element_type=f32)

    pl.when(step <= last // 2)(lambda: work(e0_ref, t0_ref))
    pl.when(step > last // 2)(lambda: work(e1_ref, t1_ref))

    @pl.when(step == last)
    def _():
        total = acc[...]
        s = s_ref[...].astype(f32)
        turn = total - s * jnp.sum(s * total, axis=-1, keepdims=True)
        dir_ref[...] = (turn * inv_ref[:, :1]).astype(bf16)
        if place is None:
            out_ref[...] = acc[...].astype(out_ref.dtype)
        else:
            half = rows // 2
            there = slice(half - place, 2 * half - place)
            here = slice(place, place + half)
            out_ref[there, :] = acc[there, :].astype(out_ref.dtype)
            out_ref[here, :] = (acc[here, :] + add_ref[...].astype(f32)).astype(out_ref.dtype)


def source_terms(dslot, rplace, block, e, cols, row_total, col_total, unit, inv, dtype, add=None, place=None):
    depth = cols[0].shape[1]
    rows, width = 512, 512
    steps = SIDE // width
    whole = lambda i, *_: (0, 0)
    early = lambda i: jnp.minimum(i, steps // 2 - 1)
    late = lambda i: jnp.maximum(i - steps // 2, 0)
    in_specs = [
        pl.BlockSpec((rows, width), lambda i, *_: (block, early(i))),
        pl.BlockSpec((rows, width), lambda i, *_: (block, late(i))),
        pl.BlockSpec((width, depth), lambda i, *_: (early(i), 0)),
        pl.BlockSpec((width, depth), lambda i, *_: (late(i), 0)),
        pl.BlockSpec((SLOTS, SHARD), whole),
        pl.BlockSpec((SLOTS, SHARD), whole),
        pl.BlockSpec((rows, depth), whole),
        pl.BlockSpec((rows, SHARD), whole),
    ]
    some = lambda v: lax.slice_in_dim(v, 4 * block, 4 * block + 4)
    args = [some(dslot), some(rplace), *e, *cols, row_total, col_total, unit, inv]
    if place is not None:
        in_specs.append(pl.BlockSpec(add.shape, whole))
        args.append(add)
    return pl.pallas_call(
        functools.partial(source_kernel, place),
        grid_spec=pltpu.PrefetchScalarGridSpec(
            num_scalar_prefetch=2,
            grid=(steps,),
            in_specs=in_specs,
            out_specs=[
                pl.BlockSpec((rows, width), lambda i, *_: (0, i)),
                pl.BlockSpec((rows, depth), whole),
                pl.BlockSpec((rows, depth), whole),
            ],
            scratch_shapes=[pltpu.VMEM((rows, depth), f32), pltpu.VMEM((rows, SHARD), f32)],
        ),
        out_shape=[
            jax.ShapeDtypeStruct((rows, SIDE), bf16),
            jax.ShapeDtypeStruct((rows, depth), dtype),
            jax.ShapeDtypeStruct((rows, depth), bf16),
        ],
        cost_estimate=pl.CostEstimate(
            flops=2 * rows * SIDE * depth, bytes_accessed=6 * rows * SIDE, transcendentals=0
        ),
        compiler_params=pltpu.CompilerParams(vmem_limit_bytes=VMEM),
        name="source_terms",
    )(*args)


def target_kernel(zplace, st_ref, t_ref, inv_ref, g0, g1, g3, g2, out_ref, dir_ref):
    step = pl.program_id(0)
    got = None
    for k, g_ref in enumerate((g0, g1, g3, g2)):
        rows = g_ref.shape[0]
        term = jnp.dot(st_ref[:, k * rows : (k + 1) * rows], g_ref[...], preferred_element_type=f32)
        got = term if got is None else got + term
    for k in range(2):
        slot = 2 * step + k
        here = slice(k * SHARD, (k + 1) * SHARD)
        part = got[:, here]
        out_ref[zplace[slot]] = part
        t = t_ref[here, :].T.astype(f32)
        turn = part - t * jnp.sum(t * part, axis=0, keepdims=True)
        dir_ref[:, here] = (turn * inv_ref[pl.ds(slot, 1), :]).astype(bf16)


def target_terms(zplace, half, rows_t, unit, inv, g):
    depth = rows_t.shape[0]
    width = 2 * SHARD
    steps = SIDE // 2 // width
    return pl.pallas_call(
        target_kernel,
        grid_spec=pltpu.PrefetchScalarGridSpec(
            num_scalar_prefetch=1,
            grid=(steps,),
            in_specs=[
                pl.BlockSpec((depth, SIDE), lambda i, *_: (0, 0)),
                pl.BlockSpec((width, depth), lambda i, *_: (i, 0)),
                pl.BlockSpec((NZ, SHARD), lambda i, *_: (0, 0)),
            ]
            + [pl.BlockSpec((512, width), lambda i, *_: (0, half * steps + i))] * 4,
            out_specs=[
                pl.BlockSpec((NZ, depth, SHARD), lambda i, *_: (0, 0, 0)),
                pl.BlockSpec((depth, width), lambda i, *_: (0, i)),
            ],
        ),
        out_shape=[
            jax.ShapeDtypeStruct((NZ, depth, SHARD), f32),
            jax.ShapeDtypeStruct((depth, SIDE // 2), bf16),
        ],
        cost_estimate=pl.CostEstimate(
            flops=SIDE * SIDE * depth, bytes_accessed=SIDE * SIDE, transcendentals=0
        ),
        compiler_params=pltpu.CompilerParams(vmem_limit_bytes=VMEM),
        name="target_terms",
    )(zplace, rows_t, unit, inv, *g)


def two_hot(shards, language):
    lang = jnp.take(language.reshape(-1, SHARD), shards, axis=0)[..., None]
    tile = (shards // (TILE // SHARD))[:, None, None] + LANGS
    lane = jnp.arange(EXTRA, dtype=jnp.int32)[None, None, :]
    hot = (lane == lang) | (lane == tile)
    return hot.astype(bf16).reshape(shards.shape[0] * SHARD, EXTRA)


def penalties(lang_allow, tile_allow):
    langs, tiles = lang_allow.shape[0], tile_allow.shape[0]
    lang = jnp.where(lang_allow == 1, 0.0, -PENALTY).astype(bf16).T
    tile = jnp.where(tile_allow == 1, 0.0, -PENALTY).astype(bf16).T
    rest = EXTRA - LANGS - tiles
    return jnp.pad(lang, ((0, EXTRA - langs), (0, EXTRA - langs))) + jnp.pad(
        tile, ((LANGS, rest), (LANGS, rest))
    )


def weight_kernel(core, *refs):
    rows, dirs, cols, dirs_t = refs[:4], refs[4:8], refs[8:10], refs[10:12]
    mine_ref, other_ref, whole = refs[12:]
    total = None
    for x, turn in zip(rows, dirs):
        term = lax.dot_general(
            x[...], turn[...], (((0,), (0,)), ((), ())), preferred_element_type=f32
        )
        total = term if total is None else total + term
    whole[...] = total
    total = None
    for x, turn in zip(cols, dirs_t):
        term = jnp.dot(turn[...], x[...], preferred_element_type=f32)
        total = term if total is None else total + term
    whole[...] += total.T
    size = mine_ref.shape[0]
    first = pl.multiple_of(core[0] * size, size)
    mine_ref[...] = whole[pl.ds(first, size), :]
    other_ref[...] = whole[pl.ds(size - first, size), :].astype(bf16)


def weight_terms(core, rows, dirs, cols, dirs_t):
    depth = rows[0].shape[1]
    count = len(rows) + len(dirs) + len(cols) + len(dirs_t)
    return pl.pallas_call(
        weight_kernel,
        in_specs=[pl.BlockSpec(memory_space=pltpu.SMEM)]
        + [pl.BlockSpec(memory_space=pltpu.VMEM)] * count,
        out_shape=[
            jax.ShapeDtypeStruct((depth // 2, depth), f32),
            jax.ShapeDtypeStruct((depth // 2, depth), bf16),
        ],
        scratch_shapes=[pltpu.VMEM((depth, depth), f32)],
        cost_estimate=pl.CostEstimate(
            flops=4 * SIDE * depth * depth, bytes_accessed=8 * SIDE * depth, transcendentals=0
        ),
        compiler_params=pltpu.CompilerParams(vmem_limit_bytes=VMEM),
        name="weight_terms",
    )(core.reshape(1), *rows, *dirs, *cols, *dirs_t)


def backward_kernel(flip, x_ref, w_ref, term0, term1, term2, out_ref):
    grad = term0[...] + term1[...] + term2[...]
    if flip:
        grad = grad.T
    raw, length = project(x_ref[...], w_ref)
    unit = raw / length
    turn = grad - unit * jnp.sum(unit * grad, axis=-1, keepdims=True)
    turn = (turn / length).astype(bf16)
    contract = (((1,), (1,)), ((), ()))
    out_ref[...] = lax.dot_general(turn, w_ref[...], contract, preferred_element_type=f32).astype(bf16)


def backward(inputs, projection, terms, flip):
    return pl.pallas_call(
        functools.partial(backward_kernel, flip),
        out_shape=jax.ShapeDtypeStruct(inputs.shape, bf16),
        compiler_params=pltpu.CompilerParams(vmem_limit_bytes=VMEM),
        name="backward",
    )(inputs, projection, *terms)


def per_device(sources, targets, projection, language, lang_allow, tile_allow):
    x, core, y, z = (lax.axis_index(name) for name in AXES)
    rel = jnp.array(REL, jnp.int32)
    first, second = jnp.tile(rel, 4), jnp.repeat(rel, 4)
    row_x = (x + jnp.where(core == 0, first, second)) % NX
    row_y = (y + jnp.where(core == 0, second, first)) % NY
    row_shard = row_x * 64 + core * 32 + row_y * 8 + z
    row_place = row_x * NY + row_y
    col_z = jnp.arange(NZ, dtype=jnp.int32)
    col_shards = [y * 64 + col_z * 8 + x * 2 + c for c in (core, 1 - core)]
    dslots = [
        jnp.max(jnp.where(row_shard[:, None] == shards[None, :], col_z[None, :], -1), axis=1)
        for shards in col_shards
    ]
    z_place = jnp.sum(
        jnp.where(
            (z + jnp.array(ZREL, jnp.int32))[None, :] % NZ == col_z[:, None], col_z[None, :], 0
        ),
        axis=1,
    )

    mine_x = lax.all_gather(targets, "z", axis=0, tiled=True)
    cost = penalties(lang_allow, tile_allow)
    row_mask = two_hot(row_shard, language)
    col_masks = [
        jnp.dot(two_hot(shards, language), cost, preferred_element_type=f32).astype(bf16)
        for shards in col_shards
    ]
    (line, p, m, q0, q1), units, invs = gather_rows(sources, projection)
    mine_x, q0, q1 = together(mine_x, q0, q1)
    other_x = send_core(mine_x)
    unit, inv, q = embed(projection, q0, q1)
    rows_x, units, invs = (line, p, m, q), (*units, unit), (*invs, inv)
    mine, mine_inv = embed(projection, mine_x, lanes=True)
    other, other_inv = embed(projection, other_x, lanes=True)

    e0, rows_t, row0, col0 = weigh(dslots[0], row_place, units, row_mask, mine, col_masks[0], False)
    e1, row1, col1 = weigh(dslots[1], row_place, units, row_mask, other, col_masks[1], True)
    row_total, col_total = sum_totals(row0 + row1, jnp.concatenate([col0, col1], axis=0))

    dslot = jnp.where(dslots[1] >= 0, dslots[1] + NZ, dslots[0])
    terms = lambda block, dtype, *add: source_terms(
        dslot,
        row_place,
        block,
        (e0, e1),
        (mine, other),
        row_total,
        col_total,
        units[block],
        invs[block],
        dtype,
        *add,
    )
    g2, o2, d2 = terms(3, bf16)
    row_place, o2 = together(row_place, o2)
    up, down = send_second(o2[:256], 1), send_second(o2[256:], -1)
    g0, o0, d0 = terms(0, f32)
    g1, o1, d1 = terms(1, f32, up, 0)
    g3, o3, d3 = terms(2, f32, down, 256)
    up, down = send_second(o1, 1), send_second(o3, -1)
    g = (g0, g1, g3, g2)
    tgt_other, other_dir = target_terms(z_place, 1, rows_t, other, other_inv, g)
    z_place, tgt_other = together(z_place, tgt_other)
    tgt_mine, mine_dir = target_terms(z_place, 0, rows_t, mine, mine_inv, g)
    weights = lambda: weight_terms(
        core, rows_x, (d0, d1, d3, d2), (mine_x, other_x), (mine_dir, other_dir)
    )
    src_parts, tgt_parts, grad_proj = scatter_rest(
        o0, up, down, tgt_mine, send_core(tgt_other), core, weights
    )
    grad_sources = backward(sources, projection, src_parts, False)
    grad_targets = backward(targets, projection, tgt_parts, True)
    return (grad_sources, grad_targets, grad_proj)


def solution(mesh):
    fine = Mesh(mesh.devices.reshape(NX, NC, NY, NZ), AXES)
    return jax.shard_map(
        per_device,
        mesh=fine,
        in_specs=(P(("x", "core", "y", "z"), None), P(("y", "z", "x", "core"), None), P(), P(), P(), P()),
        out_specs=(P(("x", "core", "y", "z"), None), P(("y", "z", "x", "core"), None), P()),
        check_vma=False,
    )
```

```python
import math
import functools
import jax
import jax.numpy as jnp
from jax import lax
from jax.experimental import pallas as pl
from jax.experimental.pallas import tpu as pltpu
from jax.sharding import Mesh, PartitionSpec as P

NX, NC, NY, NZ = 4, 2, 4, 8
AXES = ("x", "core", "y", "z")
SHARD = 128
SLOTS = 16
SIDE = SLOTS * SHARD
TILE = 512
SCALE = 20.0
MARGIN = 0.3
RATE = SCALE * math.log2(math.e)
PENALTY = 64.0
LANGS = 128
EXTRA = 256
REL = (0, 1, 3, 2)
ZREL = (0, 1, 7, 2, 6, 3, 5, 4)
VMEM = 16 * 2**20
LESS = 10 * 2**20
bf16 = jnp.bfloat16
f32 = jnp.float32


def device(x, c, y, z):
    return ((x * NC + c) * NY + y) * NZ + z


def send(value, target):
    pairs = []
    for x in range(NX):
        for c in range(NC):
            for y in range(NY):
                for z in range(NZ):
                    pairs.append((device(x, c, y, z), device(*target(x, c, y, z))))
    return lax.ppermute(value, AXES, pairs)


def send_first(value, d):
    return send(value, lambda x, c, y, z: (x, c, (y + d) % NY, z) if c else ((x + d) % NX, c, y, z))


def send_second(value, d):
    return send(value, lambda x, c, y, z: ((x + d) % NX, c, y, z) if c else (x, c, (y + d) % NY, z))


def send_z(value, d):
    return send(value, lambda x, c, y, z: (x, c, y, (z + d) % NZ))


def send_core(value):
    return send(value, lambda x, c, y, z: (x, 1 - c, y, z))


def swap(value, axis, bit):
    def target(x, c, y, z):
        place = dict(x=x, core=c, y=y, z=z)
        place[axis] ^= bit
        return tuple(place[name] for name in AXES)

    return send(value, target)


def together(*values):
    return lax.optimization_barrier(values)


def project(x, w_ref):
    raw = jnp.dot(x, w_ref[...], preferred_element_type=f32)
    length = jnp.sqrt(jnp.sum(raw * raw, axis=-1, keepdims=True) + 1e-06)
    return raw, length


def embed_kernel(lanes, count, *refs):
    pieces, w_ref, refs = refs[:count], refs[count], refs[count + 1 :]
    unit_ref, inv_ref = refs[:2]
    first = 0
    for piece in pieces:
        rows = piece.shape[0]
        here = slice(first, first + rows)
        x = piece[...]
        if count > 1:
            refs[2][here, :] = x
        raw, length = project(x, w_ref)
        unit_ref[here, :] = (raw / length).astype(bf16)
        inv = jnp.broadcast_to(1.0 / length, (rows, SHARD))
        if lanes:
            for k in range(rows // SHARD):
                inv_ref[k : k + 1, :] = inv[k * SHARD : (k + 1) * SHARD].T[:1]
        else:
            inv_ref[here, :] = inv
        first += rows


def embed(projection, *pieces, lanes=False):
    rows = sum(piece.shape[0] for piece in pieces)
    depth = projection.shape[0]
    out_shape = [
        jax.ShapeDtypeStruct((rows, depth), bf16),
        jax.ShapeDtypeStruct((rows // SHARD if lanes else rows, SHARD), f32),
    ]
    if len(pieces) > 1:
        out_shape.append(jax.ShapeDtypeStruct((rows, depth), bf16))
    return pl.pallas_call(
        functools.partial(embed_kernel, lanes, len(pieces)),
        out_shape=out_shape,
        cost_estimate=pl.CostEstimate(
            flops=2 * rows * depth * depth, bytes_accessed=4 * rows * depth, transcendentals=0
        ),
        compiler_params=pltpu.CompilerParams(vmem_limit_bytes=VMEM),
        name="embed",
    )(*pieces, projection)


def join_kernel(*refs):
    pieces, out = refs[:-1], refs[-1]
    first = 0
    for piece in pieces:
        count = piece.shape[0]
        out[first : first + count, :] = piece[...]
        first += count


def join(*pieces):
    count = sum(piece.shape[0] for piece in pieces)
    return pl.pallas_call(
        join_kernel,
        out_shape=jax.ShapeDtypeStruct((count,) + pieces[0].shape[1:], pieces[0].dtype),
        name="join",
    )(*pieces)


def gather_rows(own, projection):
    half = own.shape[0] // 2
    p, m = together(send_first(own, -1), send_first(own, 1))
    q0, q1 = together(send_first(p[:half], -1), send_first(m[half:], 1))
    line = join(own, p, m, q0, q1)
    half = line.shape[0] // 2
    p, m, *first = together(
        send_second(line, -1), send_second(line, 1), *embed(projection, line)
    )
    q0, q1, *rest = together(
        send_second(p[:half], -1),
        send_second(m[half:], 1),
        *embed(projection, p),
        *embed(projection, m),
    )
    units, invs = (first[0], rest[0], rest[2]), (first[1], rest[1], rest[3])
    return (line, p, m, q0, q1), units, invs


def plus(a, b, dtype=bf16):
    return (a.astype(f32) + b.astype(f32)).astype(dtype)


def exchange(value, axes):
    return lax.all_to_all(value, axes, split_axis=0, concat_axis=0, tiled=True)


def scatter_rest(b0, up, down, mine, other, core, weights, backwards):
    source_part, target_part = weights
    mine = mine + other
    far = mine[7].astype(bf16)
    rise, fall, weight = together(send_z(far[:384], 1), send_z(far[384:], -1), source_part())
    rise = jnp.concatenate([plus(mine[5][:384], rise), mine[5][384:].astype(bf16)], axis=0)
    fall = jnp.concatenate([mine[6][:384].astype(bf16), plus(mine[6][384:], fall)], axis=0)
    rise, fall, up, down, weight, weight_other = together(
        send_z(rise, 1), send_z(fall, -1), up, down, *target_part(weight)
    )
    half, depth = weight.shape
    part = half // (NX * NY)
    b0 = b0 + up + down
    b0, b1, b3, b2 = (b0[k * 128 : (k + 1) * 128] for k in range(4))
    weight = plus(weight, send_core(weight_other))
    up, down, rise, fall = together(
        send_first(b2[:64], 1),
        send_first(b2[64:], -1),
        send_z(plus(mine[3], rise, f32), 1),
        send_z(plus(mine[4], fall, f32), -1),
    )
    got = exchange(weight, ("x", "y")).reshape(NX * NY, part, depth)
    weight = jnp.sum(got.astype(f32), axis=0).astype(bf16)
    weight = jnp.broadcast_to(weight[None], (NZ, part, depth)).reshape(NZ * part, depth)
    b1 = jnp.concatenate([b1[:64] + up, b1[64:]], axis=0)
    b3 = jnp.concatenate([b3[:64], b3[64:] + down], axis=0)
    up, down, rise, fall = together(
        send_first(b1, 1),
        send_first(b3, -1),
        send_z(mine[1] + rise, 1),
        send_z(mine[2] + fall, -1),
    )
    got = exchange(weight, "z").reshape(NZ, part, depth)
    weight = jnp.sum(got.astype(f32), axis=0).astype(bf16)
    weight = jnp.broadcast_to(weight[None], (NX * NY, part, depth)).reshape(half, depth)
    weight, *grads = together(
        exchange(weight, ("x", "y")), *backwards((b0, up, down), (mine[0], rise, fall))
    )
    other = send_core(weight)
    low = jnp.where(core == 0, weight, other)
    high = jnp.where(core == 0, other, weight)
    return *grads, jnp.concatenate([low, high], axis=0).astype(f32)


def sum_totals(rows, cols):
    for axis, bit, other_axis, other_bit in (
        ("x", 1, "core", 1),
        ("x", 2, "z", 1),
        ("y", 1, "z", 2),
        ("y", 2, "z", 4),
    ):
        r, c = together(swap(rows, axis, bit), swap(cols, other_axis, other_bit))
        if other_axis == "core":
            c = jnp.concatenate([c[NZ:], c[:NZ]], axis=0)
        rows, cols = rows + r, cols + c
    return rows, cols


def offset_of_diagonal(rows, columns, first):
    lane = lax.broadcasted_iota(jnp.int32, (rows, columns), 1)
    return lane + first - lax.broadcasted_iota(jnp.int32, (rows, columns), 0)


def in_place(scalars, arrays):
    return [pl.BlockSpec(memory_space=pltpu.SMEM)] * scalars + [
        pl.BlockSpec(memory_space=pltpu.VMEM)
    ] * arrays


def weigh_kernel(late, dslot, rplace, *refs):
    pieces, refs = refs[:4], refs[4:]
    if late:
        sm_ref, t_ref, tm_ref, e_ref, row_ref, col_ref, s_all, acc = refs
    else:
        sm_ref, t_ref, tm_ref, e_ref, st_ref, row_ref, col_ref, s_all, acc = refs
    step = pl.program_id(0)
    rows = 2 * SHARD

    @pl.when(step == 0)
    def _():
        first = 0
        for piece in pieces:
            count = piece.shape[0]
            s_all[first : first + count, :] = piece[...]
            first += count
        acc[...] = jnp.zeros_like(acc)

    s = s_all[pl.ds(pl.multiple_of(step * rows, rows), rows), :]
    sm = sm_ref[...]
    if not late:
        st_ref[...] = s.T
    sums = [jnp.zeros((SHARD, 128), f32) for _ in range(2)]
    width = 512
    contract = (((1,), (1,)), ((), ()))
    for first in range(0, t_ref.shape[0], width):
        t = t_ref[first : first + width, :]
        tm = tm_ref[first : first + width, :]
        sim = lax.dot_general(s, t, contract, preferred_element_type=f32)
        sim += lax.dot_general(sm, tm, contract, preferred_element_type=f32)
        e = jnp.exp2(sim * RATE - RATE)
        offset = offset_of_diagonal(SHARD, width, first)
        for h in range(2):
            part = e[h * SHARD : (h + 1) * SHARD]
            part = jnp.where(offset == dslot[2 * step + h] * SHARD, 0.0, part)
            e_ref[h * SHARD : (h + 1) * SHARD, first : first + width] = part
            for k in range(0, width, 128):
                sums[h] = sums[h] + part[:, k : k + 128]
            acc[:, first : first + width] += jnp.sum(part.reshape(SHARD // 8, 8, width), axis=0)
    for h in range(2):
        slot = dslot[2 * step + h]
        place = rplace[2 * step + h]
        row_ref[pl.ds(place, 1), :] = jnp.sum(sums[h].T, axis=0, keepdims=True)

        @pl.when(slot >= 0)
        def _():
            here = pl.ds(pl.multiple_of(slot * SHARD, SHARD), SHARD)
            a = s[h * SHARD : (h + 1) * SHARD].astype(f32)
            b = t_ref[here, :].astype(f32)
            sim = jnp.sum(a * b, axis=1, keepdims=True)
            value = jnp.exp2(sim * RATE - (1.0 + MARGIN) * RATE)
            block = jnp.where(offset_of_diagonal(SHARD, SHARD, 0) == 0, value, 0.0)
            e_ref[h * SHARD : (h + 1) * SHARD, here] += block
            line = jnp.sum(block, axis=0, keepdims=True)
            row_ref[pl.ds(place, 1), :] += line
            acc[0:1, here] += line

    @pl.when(step == pl.num_programs(0) - 1)
    def _():
        total = jnp.sum(acc[...], axis=0, keepdims=True)
        for k in range(NZ):
            col_ref[k : k + 1, :] = total[:, k * SHARD : (k + 1) * SHARD]


def weigh(dslot, rplace, pieces, row_mask, cols, col_mask, late):
    depth = cols.shape[1]
    half = cols.shape[0]
    step = 2 * SHARD
    whole = lambda i, *_: (0, 0)
    in_specs = [pl.BlockSpec(v.shape, whole, pipeline_mode=pl.Buffered(1)) for v in pieces] + [
        pl.BlockSpec((step, EXTRA), lambda i, *_: (i, 0)),
        pl.BlockSpec((half, depth), whole),
        pl.BlockSpec((half, EXTRA), whole),
    ]
    out_specs = [
        pl.BlockSpec((step, half), lambda i, *_: (i, 0)),
        pl.BlockSpec((depth, step), lambda i, *_: (0, i)),
        pl.BlockSpec((SLOTS, SHARD), whole),
        pl.BlockSpec((NZ, SHARD), whole),
    ]
    out_shape = [
        jax.ShapeDtypeStruct((SIDE, half), f32),
        jax.ShapeDtypeStruct((depth, SIDE), bf16),
        jax.ShapeDtypeStruct((SLOTS, SHARD), f32),
        jax.ShapeDtypeStruct((NZ, SHARD), f32),
    ]
    if late:
        del out_specs[1], out_shape[1]
    return pl.pallas_call(
        functools.partial(weigh_kernel, late),
        grid_spec=pltpu.PrefetchScalarGridSpec(
            num_scalar_prefetch=2,
            grid=(SIDE // step,),
            in_specs=in_specs,
            out_specs=out_specs,
            scratch_shapes=[
                pltpu.VMEM((SIDE, depth), bf16),
                pltpu.VMEM((8, half), f32),
            ],
        ),
        out_shape=out_shape,
        cost_estimate=pl.CostEstimate(
            flops=2 * SIDE * half * (depth + EXTRA), bytes_accessed=4 * SIDE * half, transcendentals=SIDE * half
        ),
        compiler_params=pltpu.CompilerParams(vmem_limit_bytes=VMEM),
        name="weigh",
    )(dslot, rplace, *pieces, row_mask, cols, col_mask)


def source_kernel(block, count, dslot, rplace, e0_ref, e1_ref, t0_ref, t1_ref, rt_ref, ct_ref, *refs):
    units, invs = refs[:count], refs[count : 2 * count]
    g_ref, out_ref, dir_ref, scale = refs[2 * count :]
    rows = units[0].shape[0]
    width = 512
    shards = rows // SHARD
    eye = jnp.where(offset_of_diagonal(SHARD, SHARD, 0) == 0, SCALE, 0.0)

    @pl.loop(0, count)
    def _(step):
        base = pl.multiple_of(step * rows, rows)
        for h in range(shards):
            row = (0.5 * SCALE) / rt_ref[pl.ds(rplace[(block + step) * shards + h], 1), :]
            scale[h * SHARD : (h + 1) * SHARD, :] = jnp.broadcast_to(row, (SHARD, SHARD)).T
        total = None
        for first in range(0, SIDE, width):
            late, inner = divmod(first, SIDE // 2)
            e_ref, t_ref = (e1_ref, t1_ref) if late else (e0_ref, t0_ref)
            for k in range(first, first + width, SHARD):
                col = (0.5 * SCALE) / ct_ref[k // SHARD : k // SHARD + 1, :]
                from_e = slice(k - first + inner, k - first + inner + SHARD)
                for h in range(shards):
                    from_row = pl.ds(block * rows + base + h * SHARD, SHARD)
                    g = e_ref[from_row, from_e] * (scale[h * SHARD : (h + 1) * SHARD, :] + col)
                    flag = (dslot[(block + step) * shards + h] == k // SHARD).astype(f32)
                    g_ref[pl.ds(base + h * SHARD, SHARD), k : k + SHARD] = (g - eye * flag).astype(bf16)
            term = jnp.dot(
                g_ref[pl.ds(base, rows), first : first + width],
                t_ref[inner : inner + width, :],
                preferred_element_type=f32,
            )
            total = term if total is None else total + term
        out_ref[pl.ds(base, rows), :] = total

    for step in range(count):
        here = slice(step * rows, (step + 1) * rows)
        total = out_ref[here, :]
        s = units[step][...].astype(f32)
        turn = total - s * jnp.sum(s * total, axis=-1, keepdims=True)
        dir_ref[here, :] = (turn * invs[step][:, :1]).astype(bf16)


def source_terms(dslot, rplace, block, e, cols, row_total, col_total, units, invs):
    count = len(units)
    rows, depth = units[0].shape
    args = [dslot, rplace, *e, *cols, row_total, col_total, *units, *invs]
    return pl.pallas_call(
        functools.partial(source_kernel, block, count),
        in_specs=in_place(2, len(args) - 2),
        scratch_shapes=[pltpu.VMEM((rows, SHARD), f32)],
        out_shape=[
            jax.ShapeDtypeStruct((count * rows, SIDE), bf16),
            jax.ShapeDtypeStruct((count * rows, depth), f32),
            jax.ShapeDtypeStruct((count * rows, depth), bf16),
        ],
        cost_estimate=pl.CostEstimate(
            flops=2 * count * rows * SIDE * depth, bytes_accessed=6 * count * rows * SIDE, transcendentals=0
        ),
        compiler_params=pltpu.CompilerParams(vmem_limit_bytes=LESS),
        name="source_terms",
    )(*args)


def target_kernel(half, zplace, st_ref, t_ref, inv_ref, early, late, out_ref, dir_ref):
    width = 2 * SHARD

    @pl.loop(0, SIDE // 2 // width)
    def _(step):
        first = pl.multiple_of(step * width, width)
        got = None
        for base, g_ref in ((0, early), (early.shape[0], late)):
            term = jnp.dot(
                st_ref[:, base : base + g_ref.shape[0]],
                g_ref[:, pl.ds(half * (SIDE // 2) + first, width)],
                preferred_element_type=f32,
            )
            got = term if got is None else got + term
        for k in range(2):
            slot = 2 * step + k
            here = pl.ds(pl.multiple_of(first + k * SHARD, SHARD), SHARD)
            part = got[:, k * SHARD : (k + 1) * SHARD]
            out_ref[zplace[slot]] = part
            t = t_ref[here, :].T.astype(f32)
            turn = part - t * jnp.sum(t * part, axis=0, keepdims=True)
            dir_ref[:, here] = (turn * inv_ref[pl.ds(slot, 1), :]).astype(bf16)


def target_terms(zplace, half, rows_t, unit, inv, g):
    depth = rows_t.shape[0]
    return pl.pallas_call(
        functools.partial(target_kernel, half),
        in_specs=in_place(1, 5),
        out_shape=[
            jax.ShapeDtypeStruct((NZ, depth, SHARD), f32),
            jax.ShapeDtypeStruct((depth, SIDE // 2), bf16),
        ],
        cost_estimate=pl.CostEstimate(
            flops=SIDE * SIDE * depth, bytes_accessed=SIDE * SIDE, transcendentals=0
        ),
        compiler_params=pltpu.CompilerParams(vmem_limit_bytes=LESS),
        name="target_terms",
    )(zplace, rows_t, unit, inv, *g)


def two_hot(shards, language):
    lang = jnp.take(language.reshape(-1, SHARD), shards, axis=0)[..., None]
    tile = (shards // (TILE // SHARD))[:, None, None] + LANGS
    lane = jnp.arange(EXTRA, dtype=jnp.int32)[None, None, :]
    hot = (lane == lang) | (lane == tile)
    return hot.astype(bf16).reshape(shards.shape[0] * SHARD, EXTRA)


def penalties(lang_allow, tile_allow):
    langs, tiles = lang_allow.shape[0], tile_allow.shape[0]
    lang = jnp.where(lang_allow == 1, 0.0, -PENALTY).astype(bf16).T
    tile = jnp.where(tile_allow == 1, 0.0, -PENALTY).astype(bf16).T
    rest = EXTRA - LANGS - tiles
    return jnp.pad(lang, ((0, EXTRA - langs), (0, EXTRA - langs))) + jnp.pad(
        tile, ((LANGS, rest), (LANGS, rest))
    )


def source_weight_kernel(*refs):
    rows, early, late, out_ref = refs[:4], refs[4], refs[5], refs[6]
    total = None
    size = late.shape[0]
    dirs = [early[k * size : (k + 1) * size, :] for k in range(3)] + [late[...]]
    for x, turn in zip(rows, dirs):
        term = lax.dot_general(x[...], turn, (((0,), (0,)), ((), ())), preferred_element_type=f32)
        total = term if total is None else total + term
    out_ref[...] = total


def source_weight(rows, dirs):
    depth = rows[0].shape[1]
    return pl.pallas_call(
        source_weight_kernel,
        in_specs=in_place(0, 6),
        out_shape=jax.ShapeDtypeStruct((depth, depth), f32),
        cost_estimate=pl.CostEstimate(
            flops=2 * SIDE * depth * depth, bytes_accessed=4 * SIDE * depth, transcendentals=0
        ),
        compiler_params=pltpu.CompilerParams(vmem_limit_bytes=VMEM),
        name="source_weight",
    )(*rows, *dirs)


def target_weight_kernel(core, before, x0, x1, turn0, turn1, mine_ref, other_ref, whole):
    total = jnp.dot(turn0[...], x0[...], preferred_element_type=f32)
    total += jnp.dot(turn1[...], x1[...], preferred_element_type=f32)
    whole[...] = before[...] + total.T
    size = mine_ref.shape[0]
    first = pl.multiple_of(core[0] * size, size)
    mine_ref[...] = whole[pl.ds(first, size), :]
    other_ref[...] = whole[pl.ds(size - first, size), :].astype(bf16)


def target_weight(core, before, cols, dirs_t):
    depth = before.shape[0]
    return pl.pallas_call(
        target_weight_kernel,
        in_specs=in_place(1, 5),
        out_shape=[
            jax.ShapeDtypeStruct((depth // 2, depth), f32),
            jax.ShapeDtypeStruct((depth // 2, depth), bf16),
        ],
        scratch_shapes=[pltpu.VMEM((depth, depth), f32)],
        cost_estimate=pl.CostEstimate(
            flops=2 * SIDE * depth * depth, bytes_accessed=4 * SIDE * depth, transcendentals=0
        ),
        compiler_params=pltpu.CompilerParams(vmem_limit_bytes=VMEM),
        name="target_weight",
    )(core.reshape(1), before, *cols, *dirs_t)


def backward_kernel(flip, x_ref, w_ref, term0, term1, term2, out_ref):
    grad = term0[...] + term1[...] + term2[...]
    if flip:
        grad = grad.T
    raw, length = project(x_ref[...], w_ref)
    unit = raw / length
    turn = grad - unit * jnp.sum(unit * grad, axis=-1, keepdims=True)
    turn = (turn / length).astype(bf16)
    contract = (((1,), (1,)), ((), ()))
    out_ref[...] = lax.dot_general(turn, w_ref[...], contract, preferred_element_type=f32).astype(bf16)


def backward(inputs, projection, terms, flip):
    return pl.pallas_call(
        functools.partial(backward_kernel, flip),
        out_shape=jax.ShapeDtypeStruct(inputs.shape, bf16),
        compiler_params=pltpu.CompilerParams(vmem_limit_bytes=VMEM),
        name="backward",
    )(inputs, projection, *terms)


def per_device(sources, targets, projection, language, lang_allow, tile_allow):
    x, core, y, z = (lax.axis_index(name) for name in AXES)
    rel = jnp.array(REL, jnp.int32)
    first, second = jnp.tile(rel, 4), jnp.repeat(rel, 4)
    row_x = (x + jnp.where(core == 0, first, second)) % NX
    row_y = (y + jnp.where(core == 0, second, first)) % NY
    row_shard = row_x * 64 + core * 32 + row_y * 8 + z
    row_place = row_x * NY + row_y
    col_z = jnp.arange(NZ, dtype=jnp.int32)
    col_shards = [y * 64 + col_z * 8 + x * 2 + c for c in (core, 1 - core)]
    dslots = [
        jnp.max(jnp.where(row_shard[:, None] == shards[None, :], col_z[None, :], -1), axis=1)
        for shards in col_shards
    ]
    z_place = jnp.sum(
        jnp.where(
            (z + jnp.array(ZREL, jnp.int32))[None, :] % NZ == col_z[:, None], col_z[None, :], 0
        ),
        axis=1,
    )

    mine_x = lax.all_gather(targets, "z", axis=0, tiled=True)
    cost = penalties(lang_allow, tile_allow)
    row_mask = two_hot(row_shard, language)
    col_masks = [
        jnp.dot(two_hot(shards, language), cost, preferred_element_type=f32).astype(bf16)
        for shards in col_shards
    ]
    (line, p, m, q0, q1), units, invs = gather_rows(sources, projection)
    mine_x, q0, q1 = together(mine_x, q0, q1)
    other_x = send_core(mine_x)
    unit, inv, q = embed(projection, q0, q1)
    rows_x, units, invs = (line, p, m, q), (*units, unit), (*invs, inv)
    mine, mine_inv = embed(projection, mine_x, lanes=True)
    other, other_inv = embed(projection, other_x, lanes=True)

    e0, rows_t, row0, col0 = weigh(dslots[0], row_place, units, row_mask, mine, col_masks[0], False)
    e1, row1, col1 = weigh(dslots[1], row_place, units, row_mask, other, col_masks[1], True)
    row_total, col_total = sum_totals(row0 + row1, jnp.concatenate([col0, col1], axis=0))

    dslot = jnp.where(dslots[1] >= 0, dslots[1] + NZ, dslots[0])
    terms = functools.partial(source_terms, dslot)
    g2, o2, d2 = terms(
        row_place, 3, (e0, e1), (mine, other), row_total, col_total, units[3:], invs[3:]
    )
    row_place, o2 = together(row_place, o2.astype(bf16))
    up, down = send_second(o2[:256], 1), send_second(o2[256:], -1)
    g, o, d = terms(
        row_place, 0, (e0, e1), (mine, other), row_total, col_total, units[:3], invs[:3]
    )
    up, down, o, z_place = together(up, down, o, z_place)
    o1 = jnp.concatenate([o[512:768] + up.astype(f32), o[768:1024]], axis=0)
    o3 = jnp.concatenate([o[1024:1280], o[1280:] + down.astype(f32)], axis=0)
    up, down = send_second(o1, 1), send_second(o3, -1)
    tgt_other, other_dir = target_terms(z_place, 1, rows_t, other, other_inv, (g, g2))
    z_place, tgt_other = together(z_place, tgt_other)
    tgt_mine, mine_dir = target_terms(z_place, 0, rows_t, mine, mine_inv, (g, g2))
    weights = (
        lambda: source_weight(rows_x, (d, d2)),
        lambda before: target_weight(core, before, (mine_x, other_x), (mine_dir, other_dir)),
    )
    backwards = lambda src, tgt: (
        backward(sources, projection, src, False),
        backward(targets, projection, tgt, True),
    )
    return scatter_rest(
        o[:512], up, down, tgt_mine, send_core(tgt_other), core, weights, backwards
    )


def solution(mesh):
    fine = Mesh(mesh.devices.reshape(NX, NC, NY, NZ), AXES)
    return jax.shard_map(
        per_device,
        mesh=fine,
        in_specs=(P(("x", "core", "y", "z"), None), P(("y", "z", "x", "core"), None), P(), P(), P(), P()),
        out_specs=(P(("x", "core", "y", "z"), None), P(("y", "z", "x", "core"), None), P()),
        check_vma=False,
    )
```

```python
import math
import functools
import jax
import jax.numpy as jnp
from jax import lax
from jax.experimental import pallas as pl
from jax.experimental.pallas import tpu as pltpu
from jax.sharding import Mesh, PartitionSpec as P

NX, NC, NY, NZ = 4, 2, 4, 8
AXES = ("x", "core", "y", "z")
SHARD = 128
SLOTS = 16
SIDE = SLOTS * SHARD
TILE = 512
SCALE = 20.0
MARGIN = 0.3
RATE = SCALE * math.log2(math.e)
PENALTY = 64.0
LANGS = 128
EXTRA = 256
REL = (0, 1, 3, 2)
ZREL = (0, 1, 7, 2, 6, 3, 5, 4)
VMEM = 16 * 2**20
LESS = 10 * 2**20
bf16 = jnp.bfloat16
f32 = jnp.float32


def device(x, c, y, z):
    return ((x * NC + c) * NY + y) * NZ + z


def send(value, target):
    pairs = []
    for x in range(NX):
        for c in range(NC):
            for y in range(NY):
                for z in range(NZ):
                    pairs.append((device(x, c, y, z), device(*target(x, c, y, z))))
    return lax.ppermute(value, AXES, pairs)


def send_first(value, d):
    return send(value, lambda x, c, y, z: (x, c, (y + d) % NY, z) if c else ((x + d) % NX, c, y, z))


def send_second(value, d):
    return send(value, lambda x, c, y, z: ((x + d) % NX, c, y, z) if c else (x, c, (y + d) % NY, z))


def send_z(value, d):
    return send(value, lambda x, c, y, z: (x, c, y, (z + d) % NZ))


def send_core(value):
    return send(value, lambda x, c, y, z: (x, 1 - c, y, z))


def swap(value, axis, bit):
    def target(x, c, y, z):
        place = dict(x=x, core=c, y=y, z=z)
        place[axis] ^= bit
        return tuple(place[name] for name in AXES)

    return send(value, target)


def together(*values):
    return lax.optimization_barrier(values)


def project(x, w_ref):
    raw = jnp.dot(x, w_ref[...], preferred_element_type=f32)
    length = jnp.sqrt(jnp.sum(raw * raw, axis=-1, keepdims=True) + 1e-06)
    return raw, length


def embed_kernel(lanes, count, *refs):
    pieces, w_ref, refs = refs[:count], refs[count], refs[count + 1 :]
    unit_ref, inv_ref = refs[:2]
    first = 0
    for piece in pieces:
        rows = piece.shape[0]
        here = slice(first, first + rows)
        x = piece[...]
        if count > 1:
            refs[2][here, :] = x
        raw, length = project(x, w_ref)
        unit_ref[here, :] = (raw / length).astype(bf16)
        inv = jnp.broadcast_to(1.0 / length, (rows, SHARD))
        if lanes:
            for k in range(rows // SHARD):
                inv_ref[k : k + 1, :] = inv[k * SHARD : (k + 1) * SHARD].T[:1]
        else:
            inv_ref[here, :] = inv
        first += rows


def embed(projection, *pieces, lanes=False):
    rows = sum(piece.shape[0] for piece in pieces)
    depth = projection.shape[0]
    out_shape = [
        jax.ShapeDtypeStruct((rows, depth), bf16),
        jax.ShapeDtypeStruct((rows // SHARD if lanes else rows, SHARD), f32),
    ]
    if len(pieces) > 1:
        out_shape.append(jax.ShapeDtypeStruct((rows, depth), bf16))
    return pl.pallas_call(
        functools.partial(embed_kernel, lanes, len(pieces)),
        out_shape=out_shape,
        cost_estimate=pl.CostEstimate(
            flops=2 * rows * depth * depth, bytes_accessed=4 * rows * depth, transcendentals=0
        ),
        compiler_params=pltpu.CompilerParams(vmem_limit_bytes=VMEM),
        name="embed",
    )(*pieces, projection)


def join_kernel(*refs):
    pieces, out = refs[:-1], refs[-1]
    first = 0
    for piece in pieces:
        count = piece.shape[0]
        out[first : first + count, :] = piece[...]
        first += count


def join(*pieces):
    count = sum(piece.shape[0] for piece in pieces)
    return pl.pallas_call(
        join_kernel,
        out_shape=jax.ShapeDtypeStruct((count,) + pieces[0].shape[1:], pieces[0].dtype),
        name="join",
    )(*pieces)


def gather_rows(own, projection, *ready):
    half = own.shape[0] // 2
    p, m = together(send_first(own, -1), send_first(own, 1))
    q0, q1 = together(send_first(p[:half], -1), send_first(m[half:], 1))
    line = join(own, p, m, q0, q1)
    half = line.shape[0] // 2
    p, m, *first = together(
        send_second(line, -1), send_second(line, 1), *embed(projection, line)
    )
    q0, q1, *rest = together(
        send_second(p[:half], -1),
        send_second(m[half:], 1),
        *embed(projection, p),
        *embed(projection, m),
        *ready,
    )
    units, invs = (first[0], rest[0], rest[2]), (first[1], rest[1], rest[3])
    return (line, p, m, q0, q1), units, invs, rest[4:]


def plus(a, b, dtype=bf16):
    return (a.astype(f32) + b.astype(f32)).astype(dtype)


def exchange(value, axes):
    return lax.all_to_all(value, axes, split_axis=0, concat_axis=0, tiled=True)


def scatter_rest(b0, up, down, mine, other, core, weights, backwards):
    source_part, target_part = weights
    mine = mine + other
    far = mine[7].astype(bf16)
    rise, fall, weight = together(send_z(far[:384], 1), send_z(far[384:], -1), source_part())
    rise = jnp.concatenate([plus(mine[5][:384], rise), mine[5][384:].astype(bf16)], axis=0)
    fall = jnp.concatenate([mine[6][:384].astype(bf16), plus(mine[6][384:], fall)], axis=0)
    rise, fall, up, down, weight, weight_other = together(
        send_z(rise, 1), send_z(fall, -1), up, down, *target_part(weight)
    )
    half, depth = weight.shape
    part = half // (NX * NY)
    b0 = b0 + up + down
    b0, b1, b3, b2 = (b0[k * 128 : (k + 1) * 128] for k in range(4))
    weight = plus(weight, send_core(weight_other))
    up, down, rise, fall = together(
        send_first(b2[:64], 1),
        send_first(b2[64:], -1),
        send_z(plus(mine[3], rise, f32), 1),
        send_z(plus(mine[4], fall, f32), -1),
    )
    got = exchange(weight, ("x", "y")).reshape(NX * NY, part, depth)
    weight = jnp.sum(got.astype(f32), axis=0).astype(bf16)
    weight = jnp.broadcast_to(weight[None], (NZ, part, depth)).reshape(NZ * part, depth)
    b1 = jnp.concatenate([b1[:64] + up, b1[64:]], axis=0)
    b3 = jnp.concatenate([b3[:64], b3[64:] + down], axis=0)
    weight, b1, b3, rise, fall = together(weight, b1, b3, mine[1] + rise, mine[2] + fall)
    up, down, rise, fall = together(
        send_first(b1, 1), send_first(b3, -1), send_z(rise, 1), send_z(fall, -1)
    )
    got = exchange(weight, "z").reshape(NZ, part, depth)
    weight = jnp.sum(got.astype(f32), axis=0).astype(bf16)
    weight = jnp.broadcast_to(weight[None], (NX * NY, part, depth)).reshape(half, depth)
    weight, *grads = together(
        exchange(weight, ("x", "y")), *backwards((b0, up, down), (mine[0], rise, fall))
    )
    other = send_core(weight)
    low = jnp.where(core == 0, weight, other)
    high = jnp.where(core == 0, other, weight)
    return *grads, jnp.concatenate([low, high], axis=0).astype(f32)


def sum_totals(rows, cols):
    for axis, bit, other_axis, other_bit in (
        ("x", 1, "core", 1),
        ("x", 2, "z", 1),
        ("y", 1, "z", 2),
        ("y", 2, "z", 4),
    ):
        r, c = together(swap(rows, axis, bit), swap(cols, other_axis, other_bit))
        if other_axis == "core":
            c = jnp.concatenate([c[NZ:], c[:NZ]], axis=0)
        rows, cols = rows + r, cols + c
    return rows, cols


def offset_of_diagonal(rows, columns, first):
    lane = lax.broadcasted_iota(jnp.int32, (rows, columns), 1)
    return lane + first - lax.broadcasted_iota(jnp.int32, (rows, columns), 0)


def in_place(scalars, arrays):
    return [pl.BlockSpec(memory_space=pltpu.SMEM)] * scalars + [
        pl.BlockSpec(memory_space=pltpu.VMEM)
    ] * arrays


def weigh_kernel(late, dslot, rplace, *refs):
    pieces, refs = refs[:4], refs[4:]
    if late:
        sm_ref, t_ref, tm_ref, e_ref, row_ref, col_ref, s_all, acc = refs
    else:
        sm_ref, t_ref, tm_ref, e_ref, st_ref, row_ref, col_ref, s_all, acc = refs
    step = pl.program_id(0)
    rows = 2 * SHARD

    @pl.when(step == 0)
    def _():
        first = 0
        for piece in pieces:
            count = piece.shape[0]
            s_all[first : first + count, :] = piece[...]
            first += count
        acc[...] = jnp.zeros_like(acc)

    s = s_all[pl.ds(pl.multiple_of(step * rows, rows), rows), :]
    sm = sm_ref[...]
    if not late:
        st_ref[...] = s.T
    sums = [jnp.zeros((SHARD, 128), f32) for _ in range(2)]
    width = 512
    contract = (((1,), (1,)), ((), ()))
    for first in range(0, t_ref.shape[0], width):
        t = t_ref[first : first + width, :]
        tm = tm_ref[first : first + width, :]
        sim = lax.dot_general(s, t, contract, preferred_element_type=f32)
        sim += lax.dot_general(sm, tm, contract, preferred_element_type=f32)
        e = jnp.exp2(sim * RATE - RATE)
        offset = offset_of_diagonal(SHARD, width, first)
        for h in range(2):
            part = e[h * SHARD : (h + 1) * SHARD]
            part = jnp.where(offset == dslot[2 * step + h] * SHARD, 0.0, part)
            e_ref[h * SHARD : (h + 1) * SHARD, first : first + width] = part
            for k in range(0, width, 128):
                sums[h] = sums[h] + part[:, k : k + 128]
            acc[:, first : first + width] += jnp.sum(part.reshape(SHARD // 8, 8, width), axis=0)
    for h in range(2):
        slot = dslot[2 * step + h]
        place = rplace[2 * step + h]
        row_ref[pl.ds(place, 1), :] = jnp.sum(sums[h].T, axis=0, keepdims=True)

        @pl.when(slot >= 0)
        def _():
            here = pl.ds(pl.multiple_of(slot * SHARD, SHARD), SHARD)
            a = s[h * SHARD : (h + 1) * SHARD].astype(f32)
            b = t_ref[here, :].astype(f32)
            sim = jnp.sum(a * b, axis=1, keepdims=True)
            value = jnp.exp2(sim * RATE - (1.0 + MARGIN) * RATE)
            block = jnp.where(offset_of_diagonal(SHARD, SHARD, 0) == 0, value, 0.0)
            e_ref[h * SHARD : (h + 1) * SHARD, here] += block
            line = jnp.sum(block, axis=0, keepdims=True)
            row_ref[pl.ds(place, 1), :] += line
            acc[0:1, here] += line

    @pl.when(step == pl.num_programs(0) - 1)
    def _():
        total = jnp.sum(acc[...], axis=0, keepdims=True)
        for k in range(NZ):
            col_ref[k : k + 1, :] = total[:, k * SHARD : (k + 1) * SHARD]


def weigh(dslot, rplace, pieces, row_mask, cols, col_mask, late):
    depth = cols.shape[1]
    half = cols.shape[0]
    step = 2 * SHARD
    whole = lambda i, *_: (0, 0)
    in_specs = [pl.BlockSpec(v.shape, whole, pipeline_mode=pl.Buffered(1)) for v in pieces] + [
        pl.BlockSpec((step, EXTRA), lambda i, *_: (i, 0)),
        pl.BlockSpec((half, depth), whole),
        pl.BlockSpec((half, EXTRA), whole),
    ]
    out_specs = [
        pl.BlockSpec((step, half), lambda i, *_: (i, 0)),
        pl.BlockSpec((depth, step), lambda i, *_: (0, i)),
        pl.BlockSpec((SLOTS, SHARD), whole),
        pl.BlockSpec((NZ, SHARD), whole),
    ]
    out_shape = [
        jax.ShapeDtypeStruct((SIDE, half), f32),
        jax.ShapeDtypeStruct((depth, SIDE), bf16),
        jax.ShapeDtypeStruct((SLOTS, SHARD), f32),
        jax.ShapeDtypeStruct((NZ, SHARD), f32),
    ]
    if late:
        del out_specs[1], out_shape[1]
    return pl.pallas_call(
        functools.partial(weigh_kernel, late),
        grid_spec=pltpu.PrefetchScalarGridSpec(
            num_scalar_prefetch=2,
            grid=(SIDE // step,),
            in_specs=in_specs,
            out_specs=out_specs,
            scratch_shapes=[
                pltpu.VMEM((SIDE, depth), bf16),
                pltpu.VMEM((8, half), f32),
            ],
        ),
        out_shape=out_shape,
        cost_estimate=pl.CostEstimate(
            flops=2 * SIDE * half * (depth + EXTRA), bytes_accessed=4 * SIDE * half, transcendentals=SIDE * half
        ),
        compiler_params=pltpu.CompilerParams(vmem_limit_bytes=VMEM),
        name="weigh",
    )(dslot, rplace, *pieces, row_mask, cols, col_mask)


def source_kernel(block, count, dslot, rplace, e0_ref, e1_ref, t0_ref, t1_ref, rt_ref, ct_ref, *refs):
    units, invs = refs[:count], refs[count : 2 * count]
    g_ref, out_ref, dir_ref, scale = refs[2 * count :]
    rows = units[0].shape[0]
    width = 512
    shards = rows // SHARD
    eye = jnp.where(offset_of_diagonal(SHARD, SHARD, 0) == 0, SCALE, 0.0)

    @pl.loop(0, count)
    def _(step):
        base = pl.multiple_of(step * rows, rows)
        for h in range(shards):
            row = (0.5 * SCALE) / rt_ref[pl.ds(rplace[(block + step) * shards + h], 1), :]
            scale[h * SHARD : (h + 1) * SHARD, :] = jnp.broadcast_to(row, (SHARD, SHARD)).T
        total = None
        for first in range(0, SIDE, width):
            late, inner = divmod(first, SIDE // 2)
            e_ref, t_ref = (e1_ref, t1_ref) if late else (e0_ref, t0_ref)
            for k in range(first, first + width, SHARD):
                col = (0.5 * SCALE) / ct_ref[k // SHARD : k // SHARD + 1, :]
                from_e = slice(k - first + inner, k - first + inner + SHARD)
                for h in range(shards):
                    from_row = pl.ds(block * rows + base + h * SHARD, SHARD)
                    g = e_ref[from_row, from_e] * (scale[h * SHARD : (h + 1) * SHARD, :] + col)
                    flag = (dslot[(block + step) * shards + h] == k // SHARD).astype(f32)
                    g_ref[pl.ds(base + h * SHARD, SHARD), k : k + SHARD] = (g - eye * flag).astype(bf16)
            term = jnp.dot(
                g_ref[pl.ds(base, rows), first : first + width],
                t_ref[inner : inner + width, :],
                preferred_element_type=f32,
            )
            total = term if total is None else total + term
        out_ref[pl.ds(base, rows), :] = total

    for step in range(count):
        here = slice(step * rows, (step + 1) * rows)
        total = out_ref[here, :]
        s = units[step][...].astype(f32)
        turn = total - s * jnp.sum(s * total, axis=-1, keepdims=True)
        dir_ref[here, :] = (turn * invs[step][:, :1]).astype(bf16)


def source_terms(dslot, rplace, block, e, cols, row_total, col_total, units, invs):
    count = len(units)
    rows, depth = units[0].shape
    args = [dslot, rplace, *e, *cols, row_total, col_total, *units, *invs]
    return pl.pallas_call(
        functools.partial(source_kernel, block, count),
        in_specs=in_place(2, len(args) - 2),
        scratch_shapes=[pltpu.VMEM((rows, SHARD), f32)],
        out_shape=[
            jax.ShapeDtypeStruct((count * rows, SIDE), bf16),
            jax.ShapeDtypeStruct((count * rows, depth), f32),
            jax.ShapeDtypeStruct((count * rows, depth), bf16),
        ],
        cost_estimate=pl.CostEstimate(
            flops=2 * count * rows * SIDE * depth, bytes_accessed=6 * count * rows * SIDE, transcendentals=0
        ),
        compiler_params=pltpu.CompilerParams(vmem_limit_bytes=LESS),
        name="source_terms",
    )(*args)


def target_kernel(half, zplace, st_ref, t_ref, inv_ref, early, late, out_ref, dir_ref):
    width = 2 * SHARD

    @pl.loop(0, SIDE // 2 // width)
    def _(step):
        first = pl.multiple_of(step * width, width)
        got = None
        for base, g_ref in ((0, early), (early.shape[0], late)):
            term = jnp.dot(
                st_ref[:, base : base + g_ref.shape[0]],
                g_ref[:, pl.ds(half * (SIDE // 2) + first, width)],
                preferred_element_type=f32,
            )
            got = term if got is None else got + term
        for k in range(2):
            slot = 2 * step + k
            here = pl.ds(pl.multiple_of(first + k * SHARD, SHARD), SHARD)
            part = got[:, k * SHARD : (k + 1) * SHARD]
            out_ref[zplace[slot]] = part
            t = t_ref[here, :].T.astype(f32)
            turn = part - t * jnp.sum(t * part, axis=0, keepdims=True)
            dir_ref[:, here] = (turn * inv_ref[pl.ds(slot, 1), :]).astype(bf16)


def target_terms(zplace, half, rows_t, unit, inv, g):
    depth = rows_t.shape[0]
    return pl.pallas_call(
        functools.partial(target_kernel, half),
        in_specs=in_place(1, 5),
        out_shape=[
            jax.ShapeDtypeStruct((NZ, depth, SHARD), f32),
            jax.ShapeDtypeStruct((depth, SIDE // 2), bf16),
        ],
        cost_estimate=pl.CostEstimate(
            flops=SIDE * SIDE * depth, bytes_accessed=SIDE * SIDE, transcendentals=0
        ),
        compiler_params=pltpu.CompilerParams(vmem_limit_bytes=LESS),
        name="target_terms",
    )(zplace, rows_t, unit, inv, *g)


def two_hot(shards, language):
    lang = jnp.take(language.reshape(-1, SHARD), shards, axis=0)[..., None]
    tile = (shards // (TILE // SHARD))[:, None, None] + LANGS
    lane = jnp.arange(EXTRA, dtype=jnp.int32)[None, None, :]
    hot = (lane == lang) | (lane == tile)
    return hot.astype(bf16).reshape(shards.shape[0] * SHARD, EXTRA)


def penalties(lang_allow, tile_allow):
    langs, tiles = lang_allow.shape[0], tile_allow.shape[0]
    lang = jnp.where(lang_allow == 1, 0.0, -PENALTY).astype(bf16).T
    tile = jnp.where(tile_allow == 1, 0.0, -PENALTY).astype(bf16).T
    rest = EXTRA - LANGS - tiles
    return jnp.pad(lang, ((0, EXTRA - langs), (0, EXTRA - langs))) + jnp.pad(
        tile, ((LANGS, rest), (LANGS, rest))
    )


def source_weight_kernel(*refs):
    rows, early, late, out_ref = refs[:4], refs[4], refs[5], refs[6]
    total = None
    size = late.shape[0]
    dirs = [early[k * size : (k + 1) * size, :] for k in range(3)] + [late[...]]
    for x, turn in zip(rows, dirs):
        term = lax.dot_general(x[...], turn, (((0,), (0,)), ((), ())), preferred_element_type=f32)
        total = term if total is None else total + term
    out_ref[...] = total


def source_weight(rows, dirs):
    depth = rows[0].shape[1]
    return pl.pallas_call(
        source_weight_kernel,
        in_specs=in_place(0, 6),
        out_shape=jax.ShapeDtypeStruct((depth, depth), f32),
        cost_estimate=pl.CostEstimate(
            flops=2 * SIDE * depth * depth, bytes_accessed=4 * SIDE * depth, transcendentals=0
        ),
        compiler_params=pltpu.CompilerParams(vmem_limit_bytes=VMEM),
        name="source_weight",
    )(*rows, *dirs)


def target_weight_kernel(core, before, x0, x1, turn0, turn1, mine_ref, other_ref, whole):
    total = jnp.dot(turn0[...], x0[...], preferred_element_type=f32)
    total += jnp.dot(turn1[...], x1[...], preferred_element_type=f32)
    whole[...] = before[...] + total.T
    size = mine_ref.shape[0]
    first = pl.multiple_of(core[0] * size, size)
    mine_ref[...] = whole[pl.ds(first, size), :]
    other_ref[...] = whole[pl.ds(size - first, size), :].astype(bf16)


def target_weight(core, before, cols, dirs_t):
    depth = before.shape[0]
    return pl.pallas_call(
        target_weight_kernel,
        in_specs=in_place(1, 5),
        out_shape=[
            jax.ShapeDtypeStruct((depth // 2, depth), f32),
            jax.ShapeDtypeStruct((depth // 2, depth), bf16),
        ],
        scratch_shapes=[pltpu.VMEM((depth, depth), f32)],
        cost_estimate=pl.CostEstimate(
            flops=2 * SIDE * depth * depth, bytes_accessed=4 * SIDE * depth, transcendentals=0
        ),
        compiler_params=pltpu.CompilerParams(vmem_limit_bytes=VMEM),
        name="target_weight",
    )(core.reshape(1), before, *cols, *dirs_t)


def backward_kernel(flip, x_ref, w_ref, term0, term1, term2, out_ref):
    grad = term0[...] + term1[...] + term2[...]
    if flip:
        grad = grad.T
    raw, length = project(x_ref[...], w_ref)
    unit = raw / length
    turn = grad - unit * jnp.sum(unit * grad, axis=-1, keepdims=True)
    turn = (turn / length).astype(bf16)
    contract = (((1,), (1,)), ((), ()))
    out_ref[...] = lax.dot_general(turn, w_ref[...], contract, preferred_element_type=f32).astype(bf16)


def backward(inputs, projection, terms, flip):
    return pl.pallas_call(
        functools.partial(backward_kernel, flip),
        out_shape=jax.ShapeDtypeStruct(inputs.shape, bf16),
        compiler_params=pltpu.CompilerParams(vmem_limit_bytes=VMEM),
        name="backward",
    )(inputs, projection, *terms)


def per_device(sources, targets, projection, language, lang_allow, tile_allow):
    x, core, y, z = (lax.axis_index(name) for name in AXES)
    rel = jnp.array(REL, jnp.int32)
    first, second = jnp.tile(rel, 4), jnp.repeat(rel, 4)
    row_x = (x + jnp.where(core == 0, first, second)) % NX
    row_y = (y + jnp.where(core == 0, second, first)) % NY
    row_shard = row_x * 64 + core * 32 + row_y * 8 + z
    row_place = row_x * NY + row_y
    col_z = jnp.arange(NZ, dtype=jnp.int32)
    col_shards = [y * 64 + col_z * 8 + x * 2 + c for c in (core, 1 - core)]
    dslots = [
        jnp.max(jnp.where(row_shard[:, None] == shards[None, :], col_z[None, :], -1), axis=1)
        for shards in col_shards
    ]
    z_place = jnp.sum(
        jnp.where(
            (z + jnp.array(ZREL, jnp.int32))[None, :] % NZ == col_z[:, None], col_z[None, :], 0
        ),
        axis=1,
    )

    mine_x = lax.all_gather(targets, "z", axis=0, tiled=True)
    cost = penalties(lang_allow, tile_allow)
    row_mask = two_hot(row_shard, language)
    col_masks = [
        jnp.dot(two_hot(shards, language), cost, preferred_element_type=f32).astype(bf16)
        for shards in col_shards
    ]
    (line, p, m, q0, q1), units, invs, col_masks = gather_rows(sources, projection, *col_masks)
    mine_x, q0, q1 = together(mine_x, q0, q1)
    other_x = send_core(mine_x)
    unit, inv, q = embed(projection, q0, q1)
    rows_x, units, invs = (line, p, m, q), (*units, unit), (*invs, inv)
    mine, mine_inv = embed(projection, mine_x, lanes=True)
    other, other_inv = embed(projection, other_x, lanes=True)

    e0, rows_t, row0, col0 = weigh(dslots[0], row_place, units, row_mask, mine, col_masks[0], False)
    e1, row1, col1 = weigh(dslots[1], row_place, units, row_mask, other, col_masks[1], True)
    row_total, col_total = sum_totals(row0 + row1, jnp.concatenate([col0, col1], axis=0))

    dslot = jnp.where(dslots[1] >= 0, dslots[1] + NZ, dslots[0])
    terms = functools.partial(source_terms, dslot)
    g2, o2, d2 = terms(
        row_place, 3, (e0, e1), (mine, other), row_total, col_total, units[3:], invs[3:]
    )
    row_place, o2 = together(row_place, o2.astype(bf16))
    up, down = send_second(o2[:256], 1), send_second(o2[256:], -1)
    g, o, d = terms(
        row_place, 0, (e0, e1), (mine, other), row_total, col_total, units[:3], invs[:3]
    )
    up, down, o, z_place = together(up, down, o, z_place)
    o1 = jnp.concatenate([o[512:768] + up.astype(f32), o[768:1024]], axis=0)
    o3 = jnp.concatenate([o[1024:1280], o[1280:] + down.astype(f32)], axis=0)
    up, down = send_second(o1, 1), send_second(o3, -1)
    tgt_other, other_dir = target_terms(z_place, 1, rows_t, other, other_inv, (g, g2))
    z_place, tgt_other = together(z_place, tgt_other)
    tgt_mine, mine_dir = target_terms(z_place, 0, rows_t, mine, mine_inv, (g, g2))
    weights = (
        lambda: source_weight(rows_x, (d, d2)),
        lambda before: target_weight(core, before, (mine_x, other_x), (mine_dir, other_dir)),
    )
    backwards = lambda src, tgt: (
        backward(sources, projection, src, False),
        backward(targets, projection, tgt, True),
    )
    return scatter_rest(
        o[:512], up, down, tgt_mine, send_core(tgt_other), core, weights, backwards
    )


def solution(mesh):
    fine = Mesh(mesh.devices.reshape(NX, NC, NY, NZ), AXES)
    return jax.shard_map(
        per_device,
        mesh=fine,
        in_specs=(P(("x", "core", "y", "z"), None), P(("y", "z", "x", "core"), None), P(), P(), P(), P()),
        out_specs=(P(("x", "core", "y", "z"), None), P(("y", "z", "x", "core"), None), P()),
        check_vma=False,
    )
```

```python
import math
import functools
import jax
import jax.numpy as jnp
from jax import lax
from jax.experimental import pallas as pl
from jax.experimental.pallas import tpu as pltpu
from jax.sharding import Mesh, PartitionSpec as P

NX, NC, NY, NZ = 4, 2, 4, 8
AXES = ("x", "core", "y", "z")
SHARD = 128
SLOTS = 16
SIDE = SLOTS * SHARD
TILE = 512
SCALE = 20.0
MARGIN = 0.3
RATE = SCALE * math.log2(math.e)
PENALTY = 64.0
LANGS = 128
EXTRA = 256
REL = (0, 1, 3, 2)
ZREL = (0, 1, 7, 2, 6, 3, 5, 4)
VMEM = 16 * 2**20
LESS = 10 * 2**20
bf16 = jnp.bfloat16
f32 = jnp.float32


def device(x, c, y, z):
    return ((x * NC + c) * NY + y) * NZ + z


def send(value, target):
    pairs = []
    for x in range(NX):
        for c in range(NC):
            for y in range(NY):
                for z in range(NZ):
                    pairs.append((device(x, c, y, z), device(*target(x, c, y, z))))
    return lax.ppermute(value, AXES, pairs)


def send_first(value, d):
    return send(value, lambda x, c, y, z: (x, c, (y + d) % NY, z) if c else ((x + d) % NX, c, y, z))


def send_second(value, d):
    return send(value, lambda x, c, y, z: ((x + d) % NX, c, y, z) if c else (x, c, (y + d) % NY, z))


def send_z(value, d):
    return send(value, lambda x, c, y, z: (x, c, y, (z + d) % NZ))


def send_core(value):
    return send(value, lambda x, c, y, z: (x, 1 - c, y, z))


def swap(value, axis, bit):
    def target(x, c, y, z):
        place = dict(x=x, core=c, y=y, z=z)
        place[axis] ^= bit
        return tuple(place[name] for name in AXES)

    return send(value, target)


def together(*values):
    return lax.optimization_barrier(values)


def project(x, w_ref):
    raw = jnp.dot(x, w_ref[...], preferred_element_type=f32)
    length = jnp.sqrt(jnp.sum(raw * raw, axis=-1, keepdims=True) + 1e-06)
    return raw, length


def embed_kernel(lanes, count, *refs):
    pieces, w_ref, refs = refs[:count], refs[count], refs[count + 1 :]
    unit_ref, inv_ref = refs[:2]
    first = 0
    for piece in pieces:
        rows = piece.shape[0]
        here = slice(first, first + rows)
        x = piece[...]
        if count > 1:
            refs[2][here, :] = x
        raw, length = project(x, w_ref)
        unit_ref[here, :] = (raw / length).astype(bf16)
        inv = jnp.broadcast_to(1.0 / length, (rows, SHARD))
        if lanes:
            for k in range(rows // SHARD):
                inv_ref[k : k + 1, :] = inv[k * SHARD : (k + 1) * SHARD].T[:1]
        else:
            inv_ref[here, :] = inv
        first += rows


def embed(projection, *pieces, lanes=False):
    rows = sum(piece.shape[0] for piece in pieces)
    depth = projection.shape[0]
    out_shape = [
        jax.ShapeDtypeStruct((rows, depth), bf16),
        jax.ShapeDtypeStruct((rows // SHARD if lanes else rows, SHARD), f32),
    ]
    if len(pieces) > 1:
        out_shape.append(jax.ShapeDtypeStruct((rows, depth), bf16))
    return pl.pallas_call(
        functools.partial(embed_kernel, lanes, len(pieces)),
        out_shape=out_shape,
        cost_estimate=pl.CostEstimate(
            flops=2 * rows * depth * depth, bytes_accessed=4 * rows * depth, transcendentals=0
        ),
        compiler_params=pltpu.CompilerParams(vmem_limit_bytes=VMEM),
        name="embed",
    )(*pieces, projection)


def join_kernel(*refs):
    pieces, out = refs[:-1], refs[-1]
    first = 0
    for piece in pieces:
        count = piece.shape[0]
        out[first : first + count, :] = piece[...]
        first += count


def join(*pieces):
    count = sum(piece.shape[0] for piece in pieces)
    return pl.pallas_call(
        join_kernel,
        out_shape=jax.ShapeDtypeStruct((count,) + pieces[0].shape[1:], pieces[0].dtype),
        name="join",
    )(*pieces)


def gather_rows(own, projection):
    half = own.shape[0] // 2
    p, m = together(send_first(own, -1), send_first(own, 1))
    q0, q1 = together(send_first(p[:half], -1), send_first(m[half:], 1))
    line = join(own, p, m, q0, q1)
    half = line.shape[0] // 2
    p, m, *first = together(
        send_second(line, -1), send_second(line, 1), *embed(projection, line)
    )
    q0, q1, *rest = together(
        send_second(p[:half], -1),
        send_second(m[half:], 1),
        *embed(projection, p),
        *embed(projection, m),
    )
    units, invs = (first[0], rest[0], rest[2]), (first[1], rest[1], rest[3])
    return (line, p, m, q0, q1), units, invs


def plus(a, b, dtype=bf16):
    return (a.astype(f32) + b.astype(f32)).astype(dtype)


def exchange(value, axes):
    return lax.all_to_all(value, axes, split_axis=0, concat_axis=0, tiled=True)


def scatter_rest(b0, up, down, mine, other, core, weights, backwards):
    source_part, target_part = weights
    mine = mine + other
    far = mine[7].astype(bf16)
    rise, fall, weight = together(send_z(far[:384], 1), send_z(far[384:], -1), source_part())
    rise = jnp.concatenate([plus(mine[5][:384], rise), mine[5][384:].astype(bf16)], axis=0)
    fall = jnp.concatenate([mine[6][:384].astype(bf16), plus(mine[6][384:], fall)], axis=0)
    rise, fall, up, down, weight, weight_other = together(
        send_z(rise, 1), send_z(fall, -1), up, down, *target_part(weight)
    )
    half, depth = weight.shape
    part = half // (NX * NY)
    b0 = b0 + up + down
    b0, b1, b3, b2 = (b0[k * 128 : (k + 1) * 128] for k in range(4))
    weight = plus(weight, send_core(weight_other))
    rise, fall = together(
        send_z(plus(mine[3], rise, f32), 1), send_z(plus(mine[4], fall, f32), -1)
    )
    up, down = together(send_first(b2[:64], 1), send_first(b2[64:], -1))
    got = exchange(weight, ("x", "y")).reshape(NX * NY, part, depth)
    weight = jnp.sum(got.astype(f32), axis=0).astype(bf16)
    weight = jnp.broadcast_to(weight[None], (NZ, part, depth)).reshape(NZ * part, depth)
    b1 = jnp.concatenate([b1[:64] + up, b1[64:]], axis=0)
    b3 = jnp.concatenate([b3[:64], b3[64:] + down], axis=0)
    rise, fall = together(send_z(mine[1] + rise, 1), send_z(mine[2] + fall, -1))
    up, down = together(send_first(b1, 1), send_first(b3, -1))
    got = exchange(weight, "z").reshape(NZ, part, depth)
    weight = jnp.sum(got.astype(f32), axis=0).astype(bf16)
    weight = jnp.broadcast_to(weight[None], (NX * NY, part, depth)).reshape(half, depth)
    weight, *grads = together(
        exchange(weight, ("x", "y")), *backwards((b0, up, down), (mine[0], rise, fall))
    )
    other = send_core(weight)
    low = jnp.where(core == 0, weight, other)
    high = jnp.where(core == 0, other, weight)
    return *grads, jnp.concatenate([low, high], axis=0).astype(f32)


def sum_totals(rows, cols):
    for axis, bit, other_axis, other_bit in (
        ("x", 1, "core", 1),
        ("x", 2, "z", 1),
        ("y", 1, "z", 2),
        ("y", 2, "z", 4),
    ):
        r, c = together(swap(rows, axis, bit), swap(cols, other_axis, other_bit))
        if other_axis == "core":
            c = jnp.concatenate([c[NZ:], c[:NZ]], axis=0)
        rows, cols = rows + r, cols + c
    return rows, cols


def offset_of_diagonal(rows, columns, first):
    lane = lax.broadcasted_iota(jnp.int32, (rows, columns), 1)
    return lane + first - lax.broadcasted_iota(jnp.int32, (rows, columns), 0)


def in_place(scalars, arrays):
    return [pl.BlockSpec(memory_space=pltpu.SMEM)] * scalars + [
        pl.BlockSpec(memory_space=pltpu.VMEM)
    ] * arrays


def weigh_kernel(late, dslot, rplace, *refs):
    pieces, refs = refs[:4], refs[4:]
    if late:
        sm_ref, t_ref, tm_ref, e_ref, row_ref, col_ref, s_all, acc = refs
    else:
        sm_ref, t_ref, tm_ref, e_ref, st_ref, row_ref, col_ref, s_all, acc = refs
    step = pl.program_id(0)
    rows = 2 * SHARD

    @pl.when(step == 0)
    def _():
        first = 0
        for piece in pieces:
            count = piece.shape[0]
            s_all[first : first + count, :] = piece[...]
            first += count
        acc[...] = jnp.zeros_like(acc)

    s = s_all[pl.ds(pl.multiple_of(step * rows, rows), rows), :]
    sm = sm_ref[...]
    if not late:
        st_ref[...] = s.T
    sums = [jnp.zeros((SHARD, 128), f32) for _ in range(2)]
    width = 512
    contract = (((1,), (1,)), ((), ()))
    for first in range(0, t_ref.shape[0], width):
        t = t_ref[first : first + width, :]
        tm = tm_ref[first : first + width, :]
        sim = lax.dot_general(s, t, contract, preferred_element_type=f32)
        sim += lax.dot_general(sm, tm, contract, preferred_element_type=f32)
        e = jnp.exp2(sim * RATE - RATE)
        offset = offset_of_diagonal(SHARD, width, first)
        for h in range(2):
            part = e[h * SHARD : (h + 1) * SHARD]
            part = jnp.where(offset == dslot[2 * step + h] * SHARD, 0.0, part)
            e_ref[h * SHARD : (h + 1) * SHARD, first : first + width] = part
            for k in range(0, width, 128):
                sums[h] = sums[h] + part[:, k : k + 128]
            acc[:, first : first + width] += jnp.sum(part.reshape(SHARD // 8, 8, width), axis=0)
    for h in range(2):
        slot = dslot[2 * step + h]
        place = rplace[2 * step + h]
        row_ref[pl.ds(place, 1), :] = jnp.sum(sums[h].T, axis=0, keepdims=True)

        @pl.when(slot >= 0)
        def _():
            here = pl.ds(pl.multiple_of(slot * SHARD, SHARD), SHARD)
            a = s[h * SHARD : (h + 1) * SHARD].astype(f32)
            b = t_ref[here, :].astype(f32)
            sim = jnp.sum(a * b, axis=1, keepdims=True)
            value = jnp.exp2(sim * RATE - (1.0 + MARGIN) * RATE)
            block = jnp.where(offset_of_diagonal(SHARD, SHARD, 0) == 0, value, 0.0)
            e_ref[h * SHARD : (h + 1) * SHARD, here] += block
            line = jnp.sum(block, axis=0, keepdims=True)
            row_ref[pl.ds(place, 1), :] += line
            acc[0:1, here] += line

    @pl.when(step == pl.num_programs(0) - 1)
    def _():
        total = jnp.sum(acc[...], axis=0, keepdims=True)
        for k in range(NZ):
            col_ref[k : k + 1, :] = total[:, k * SHARD : (k + 1) * SHARD]


def weigh(dslot, rplace, pieces, row_mask, cols, col_mask, late):
    depth = cols.shape[1]
    half = cols.shape[0]
    step = 2 * SHARD
    whole = lambda i, *_: (0, 0)
    in_specs = [pl.BlockSpec(v.shape, whole, pipeline_mode=pl.Buffered(1)) for v in pieces] + [
        pl.BlockSpec((step, EXTRA), lambda i, *_: (i, 0)),
        pl.BlockSpec((half, depth), whole),
        pl.BlockSpec((half, EXTRA), whole),
    ]
    out_specs = [
        pl.BlockSpec((step, half), lambda i, *_: (i, 0)),
        pl.BlockSpec((depth, step), lambda i, *_: (0, i)),
        pl.BlockSpec((SLOTS, SHARD), whole),
        pl.BlockSpec((NZ, SHARD), whole),
    ]
    out_shape = [
        jax.ShapeDtypeStruct((SIDE, half), f32),
        jax.ShapeDtypeStruct((depth, SIDE), bf16),
        jax.ShapeDtypeStruct((SLOTS, SHARD), f32),
        jax.ShapeDtypeStruct((NZ, SHARD), f32),
    ]
    if late:
        del out_specs[1], out_shape[1]
    return pl.pallas_call(
        functools.partial(weigh_kernel, late),
        grid_spec=pltpu.PrefetchScalarGridSpec(
            num_scalar_prefetch=2,
            grid=(SIDE // step,),
            in_specs=in_specs,
            out_specs=out_specs,
            scratch_shapes=[
                pltpu.VMEM((SIDE, depth), bf16),
                pltpu.VMEM((8, half), f32),
            ],
        ),
        out_shape=out_shape,
        cost_estimate=pl.CostEstimate(
            flops=2 * SIDE * half * (depth + EXTRA), bytes_accessed=4 * SIDE * half, transcendentals=SIDE * half
        ),
        compiler_params=pltpu.CompilerParams(vmem_limit_bytes=VMEM),
        name="weigh",
    )(dslot, rplace, *pieces, row_mask, cols, col_mask)


def source_kernel(block, count, dslot, rplace, e0_ref, e1_ref, t0_ref, t1_ref, rt_ref, ct_ref, *refs):
    units, invs = refs[:count], refs[count : 2 * count]
    g_ref, out_ref, dir_ref, scale = refs[2 * count :]
    rows = units[0].shape[0]
    width = 512
    shards = rows // SHARD
    eye = jnp.where(offset_of_diagonal(SHARD, SHARD, 0) == 0, SCALE, 0.0)

    @pl.loop(0, count)
    def _(step):
        base = pl.multiple_of(step * rows, rows)
        for h in range(shards):
            row = (0.5 * SCALE) / rt_ref[pl.ds(rplace[(block + step) * shards + h], 1), :]
            scale[h * SHARD : (h + 1) * SHARD, :] = jnp.broadcast_to(row, (SHARD, SHARD)).T
        total = None
        for first in range(0, SIDE, width):
            late, inner = divmod(first, SIDE // 2)
            e_ref, t_ref = (e1_ref, t1_ref) if late else (e0_ref, t0_ref)
            for k in range(first, first + width, SHARD):
                col = (0.5 * SCALE) / ct_ref[k // SHARD : k // SHARD + 1, :]
                from_e = slice(k - first + inner, k - first + inner + SHARD)
                for h in range(shards):
                    from_row = pl.ds(block * rows + base + h * SHARD, SHARD)
                    g = e_ref[from_row, from_e] * (scale[h * SHARD : (h + 1) * SHARD, :] + col)
                    flag = (dslot[(block + step) * shards + h] == k // SHARD).astype(f32)
                    g_ref[pl.ds(base + h * SHARD, SHARD), k : k + SHARD] = (g - eye * flag).astype(bf16)
            term = jnp.dot(
                g_ref[pl.ds(base, rows), first : first + width],
                t_ref[inner : inner + width, :],
                preferred_element_type=f32,
            )
            total = term if total is None else total + term
        out_ref[pl.ds(base, rows), :] = total

    for step in range(count):
        here = slice(step * rows, (step + 1) * rows)
        total = out_ref[here, :]
        s = units[step][...].astype(f32)
        turn = total - s * jnp.sum(s * total, axis=-1, keepdims=True)
        dir_ref[here, :] = (turn * invs[step][:, :1]).astype(bf16)


def source_terms(dslot, rplace, block, e, cols, row_total, col_total, units, invs):
    count = len(units)
    rows, depth = units[0].shape
    args = [dslot, rplace, *e, *cols, row_total, col_total, *units, *invs]
    return pl.pallas_call(
        functools.partial(source_kernel, block, count),
        in_specs=in_place(2, len(args) - 2),
        scratch_shapes=[pltpu.VMEM((rows, SHARD), f32)],
        out_shape=[
            jax.ShapeDtypeStruct((count * rows, SIDE), bf16),
            jax.ShapeDtypeStruct((count * rows, depth), f32),
            jax.ShapeDtypeStruct((count * rows, depth), bf16),
        ],
        cost_estimate=pl.CostEstimate(
            flops=2 * count * rows * SIDE * depth, bytes_accessed=6 * count * rows * SIDE, transcendentals=0
        ),
        compiler_params=pltpu.CompilerParams(vmem_limit_bytes=LESS),
        name="source_terms",
    )(*args)


def target_kernel(half, zplace, st_ref, t_ref, inv_ref, early, late, out_ref, dir_ref):
    width = 2 * SHARD

    @pl.loop(0, SIDE // 2 // width)
    def _(step):
        first = pl.multiple_of(step * width, width)
        got = None
        for base, g_ref in ((0, early), (early.shape[0], late)):
            term = jnp.dot(
                st_ref[:, base : base + g_ref.shape[0]],
                g_ref[:, pl.ds(half * (SIDE // 2) + first, width)],
                preferred_element_type=f32,
            )
            got = term if got is None else got + term
        for k in range(2):
            slot = 2 * step + k
            here = pl.ds(pl.multiple_of(first + k * SHARD, SHARD), SHARD)
            part = got[:, k * SHARD : (k + 1) * SHARD]
            out_ref[zplace[slot]] = part
            t = t_ref[here, :].T.astype(f32)
            turn = part - t * jnp.sum(t * part, axis=0, keepdims=True)
            dir_ref[:, here] = (turn * inv_ref[pl.ds(slot, 1), :]).astype(bf16)


def target_terms(zplace, half, rows_t, unit, inv, g):
    depth = rows_t.shape[0]
    return pl.pallas_call(
        functools.partial(target_kernel, half),
        in_specs=in_place(1, 5),
        out_shape=[
            jax.ShapeDtypeStruct((NZ, depth, SHARD), f32),
            jax.ShapeDtypeStruct((depth, SIDE // 2), bf16),
        ],
        cost_estimate=pl.CostEstimate(
            flops=SIDE * SIDE * depth, bytes_accessed=SIDE * SIDE, transcendentals=0
        ),
        compiler_params=pltpu.CompilerParams(vmem_limit_bytes=LESS),
        name="target_terms",
    )(zplace, rows_t, unit, inv, *g)


def two_hot(shards, language):
    lang = jnp.take(language.reshape(-1, SHARD), shards, axis=0)[..., None]
    tile = (shards // (TILE // SHARD))[:, None, None] + LANGS
    lane = jnp.arange(EXTRA, dtype=jnp.int32)[None, None, :]
    hot = (lane == lang) | (lane == tile)
    return hot.astype(bf16).reshape(shards.shape[0] * SHARD, EXTRA)


def penalties(lang_allow, tile_allow):
    langs, tiles = lang_allow.shape[0], tile_allow.shape[0]
    lang = jnp.where(lang_allow == 1, 0.0, -PENALTY).astype(bf16).T
    tile = jnp.where(tile_allow == 1, 0.0, -PENALTY).astype(bf16).T
    rest = EXTRA - LANGS - tiles
    return jnp.pad(lang, ((0, EXTRA - langs), (0, EXTRA - langs))) + jnp.pad(
        tile, ((LANGS, rest), (LANGS, rest))
    )


def source_weight_kernel(*refs):
    rows, early, late, out_ref = refs[:4], refs[4], refs[5], refs[6]
    total = None
    size = late.shape[0]
    dirs = [early[k * size : (k + 1) * size, :] for k in range(3)] + [late[...]]
    for x, turn in zip(rows, dirs):
        term = lax.dot_general(x[...], turn, (((0,), (0,)), ((), ())), preferred_element_type=f32)
        total = term if total is None else total + term
    out_ref[...] = total


def source_weight(rows, dirs):
    depth = rows[0].shape[1]
    return pl.pallas_call(
        source_weight_kernel,
        in_specs=in_place(0, 6),
        out_shape=jax.ShapeDtypeStruct((depth, depth), f32),
        cost_estimate=pl.CostEstimate(
            flops=2 * SIDE * depth * depth, bytes_accessed=4 * SIDE * depth, transcendentals=0
        ),
        compiler_params=pltpu.CompilerParams(vmem_limit_bytes=VMEM),
        name="source_weight",
    )(*rows, *dirs)


def target_weight_kernel(core, before, x0, x1, turn0, turn1, mine_ref, other_ref, whole):
    total = jnp.dot(turn0[...], x0[...], preferred_element_type=f32)
    total += jnp.dot(turn1[...], x1[...], preferred_element_type=f32)
    whole[...] = before[...] + total.T
    size = mine_ref.shape[0]
    first = pl.multiple_of(core[0] * size, size)
    mine_ref[...] = whole[pl.ds(first, size), :]
    other_ref[...] = whole[pl.ds(size - first, size), :].astype(bf16)


def target_weight(core, before, cols, dirs_t):
    depth = before.shape[0]
    return pl.pallas_call(
        target_weight_kernel,
        in_specs=in_place(1, 5),
        out_shape=[
            jax.ShapeDtypeStruct((depth // 2, depth), f32),
            jax.ShapeDtypeStruct((depth // 2, depth), bf16),
        ],
        scratch_shapes=[pltpu.VMEM((depth, depth), f32)],
        cost_estimate=pl.CostEstimate(
            flops=2 * SIDE * depth * depth, bytes_accessed=4 * SIDE * depth, transcendentals=0
        ),
        compiler_params=pltpu.CompilerParams(vmem_limit_bytes=VMEM),
        name="target_weight",
    )(core.reshape(1), before, *cols, *dirs_t)


def backward_kernel(flip, x_ref, w_ref, term0, term1, term2, out_ref):
    grad = term0[...] + term1[...] + term2[...]
    if flip:
        grad = grad.T
    raw, length = project(x_ref[...], w_ref)
    unit = raw / length
    turn = grad - unit * jnp.sum(unit * grad, axis=-1, keepdims=True)
    turn = (turn / length).astype(bf16)
    contract = (((1,), (1,)), ((), ()))
    out_ref[...] = lax.dot_general(turn, w_ref[...], contract, preferred_element_type=f32).astype(bf16)


def backward(inputs, projection, terms, flip):
    return pl.pallas_call(
        functools.partial(backward_kernel, flip),
        out_shape=jax.ShapeDtypeStruct(inputs.shape, bf16),
        compiler_params=pltpu.CompilerParams(vmem_limit_bytes=VMEM),
        name="backward",
    )(inputs, projection, *terms)


def per_device(sources, targets, projection, language, lang_allow, tile_allow):
    x, core, y, z = (lax.axis_index(name) for name in AXES)
    rel = jnp.array(REL, jnp.int32)
    first, second = jnp.tile(rel, 4), jnp.repeat(rel, 4)
    row_x = (x + jnp.where(core == 0, first, second)) % NX
    row_y = (y + jnp.where(core == 0, second, first)) % NY
    row_shard = row_x * 64 + core * 32 + row_y * 8 + z
    row_place = row_x * NY + row_y
    col_z = jnp.arange(NZ, dtype=jnp.int32)
    col_shards = [y * 64 + col_z * 8 + x * 2 + c for c in (core, 1 - core)]
    dslots = [
        jnp.max(jnp.where(row_shard[:, None] == shards[None, :], col_z[None, :], -1), axis=1)
        for shards in col_shards
    ]
    z_place = jnp.sum(
        jnp.where(
            (z + jnp.array(ZREL, jnp.int32))[None, :] % NZ == col_z[:, None], col_z[None, :], 0
        ),
        axis=1,
    )

    mine_x = lax.all_gather(targets, "z", axis=0, tiled=True)
    cost = penalties(lang_allow, tile_allow)
    row_mask = two_hot(row_shard, language)
    col_masks = [
        jnp.dot(two_hot(shards, language), cost, preferred_element_type=f32).astype(bf16)
        for shards in col_shards
    ]
    (line, p, m, q0, q1), units, invs = gather_rows(sources, projection)
    mine_x, q0, q1 = together(mine_x, q0, q1)
    other_x = send_core(mine_x)
    unit, inv, q = embed(projection, q0, q1)
    rows_x, units, invs = (line, p, m, q), (*units, unit), (*invs, inv)
    mine, mine_inv = embed(projection, mine_x, lanes=True)
    other, other_inv = embed(projection, other_x, lanes=True)

    e0, rows_t, row0, col0 = weigh(dslots[0], row_place, units, row_mask, mine, col_masks[0], False)
    e1, row1, col1 = weigh(dslots[1], row_place, units, row_mask, other, col_masks[1], True)
    row_total, col_total = sum_totals(row0 + row1, jnp.concatenate([col0, col1], axis=0))

    dslot = jnp.where(dslots[1] >= 0, dslots[1] + NZ, dslots[0])
    terms = functools.partial(source_terms, dslot)
    g2, o2, d2 = terms(
        row_place, 3, (e0, e1), (mine, other), row_total, col_total, units[3:], invs[3:]
    )
    row_place, o2 = together(row_place, o2.astype(bf16))
    up, down = send_second(o2[:256], 1), send_second(o2[256:], -1)
    g, o, d = terms(
        row_place, 0, (e0, e1), (mine, other), row_total, col_total, units[:3], invs[:3]
    )
    up, down, o, z_place = together(up, down, o, z_place)
    o1 = jnp.concatenate([o[512:768] + up.astype(f32), o[768:1024]], axis=0)
    o3 = jnp.concatenate([o[1024:1280], o[1280:] + down.astype(f32)], axis=0)
    up, down = send_second(o1, 1), send_second(o3, -1)
    tgt_other, other_dir = target_terms(z_place, 1, rows_t, other, other_inv, (g, g2))
    z_place, tgt_other = together(z_place, tgt_other)
    tgt_mine, mine_dir = target_terms(z_place, 0, rows_t, mine, mine_inv, (g, g2))
    weights = (
        lambda: source_weight(rows_x, (d, d2)),
        lambda before: target_weight(core, before, (mine_x, other_x), (mine_dir, other_dir)),
    )
    backwards = lambda src, tgt: (
        backward(sources, projection, src, False),
        backward(targets, projection, tgt, True),
    )
    return scatter_rest(
        o[:512], up, down, tgt_mine, send_core(tgt_other), core, weights, backwards
    )


def solution(mesh):
    fine = Mesh(mesh.devices.reshape(NX, NC, NY, NZ), AXES)
    return jax.shard_map(
        per_device,
        mesh=fine,
        in_specs=(P(("x", "core", "y", "z"), None), P(("y", "z", "x", "core"), None), P(), P(), P(), P()),
        out_specs=(P(("x", "core", "y", "z"), None), P(("y", "z", "x", "core"), None), P()),
        check_vma=False,
    )
```
